512 devices in a mesh: sx: 32 (over y, x, core), sy: 16 (over z).
Axes of the slice: x: 4, y: 4, z: 16, core: 2. Of those that a mesh axis runs over, the one named last changes fastest.
Arguments:
- inputs: bfloat16 [65536, 4096], P(('sx', 'sy')), may hold values from -6 to 6
- keys_in: bfloat16 [65536, 128], P(('sx', 'sy')), may hold values from -6 to 6
- queries: bfloat16 [65536, 128], P(('sx', 'sy')), may hold values from -6 to 6
- step_sizes: float32 [65536, 64], P(('sx', 'sy')), may hold values from 0.01 to 0.1
- level_weights: float32 [20, 64], replicated, may hold values from 0.3 to 3
- skip_gain: float32 [64], replicated, may hold values from 0.5 to 1.5
Outputs:
- outputs: bfloat16 [65536, 4096], P(('sx', 'sy'))
The draws below stay inside these ranges and needn't reach their ends.
All inputs are finite; a program needn't handle non-finite values.
Results may differ from the reference program's by a relative error of at most 0.005.
Values sent between devices are 32-bit elements; how exact they have to be, the bound alone decides.
A program may use at most 64 MiB of HBM per device.

```python
import math
import jax
import jax.numpy as jnp
from jax import lax

HEADS = 64
HEAD_DIM = 64
STATE = 128
STRETCH = 64
LEVEL_CAP = 20
TOKENS = 65536


def block_scale(stream_key, dims, pieces, smallest, largest):
    gain, own = 1.0, jax.random.fold_in(stream_key, 6)
    for position, parts in pieces:
        steps = jnp.exp(jax.random.uniform(jax.random.fold_in(own, position), (parts,), jnp.float32, smallest / len(pieces), largest / len(pieces)))
        gain = gain * jnp.repeat(steps, dims[position] // parts).reshape([-1 if axis == position else 1 for axis in range(len(dims))])
    return gain


def normal_values(stream_key, shape, deviation, most, split=(), held_as=jnp.bfloat16):
    drawn = deviation * jax.random.normal(stream_key, shape, jnp.float32)
    if split:
        drawn = drawn * block_scale(stream_key, shape, split, -0.22, 0.18)
    return jnp.clip(drawn, -most, most).astype(held_as)


def setup_inputs(seed: int = 0) -> dict:
    key_list = jax.random.split(jax.random.key(seed), 7)
    return {
        "inputs": normal_values(key_list[0], (TOKENS, HEADS * HEAD_DIM), 1.0, 6.0, ((0, 512),)),
        "keys_in": normal_values(key_list[1], (TOKENS, STATE), 1.0, 6.0, ((0, 512),)),
        "queries": normal_values(key_list[2], (TOKENS, STATE), 1.0, 6.0, ((0, 512),)),
        "step_sizes": jnp.clip(jnp.exp(math.log(0.1) - 2.3025851 * jax.random.uniform(key_list[3], (TOKENS, HEADS), jnp.float32) ** block_scale(key_list[3], (TOKENS, HEADS), ((0, 512),), -0.2, 0.2)), 0.01, 0.1),
        "level_weights": jnp.clip(jnp.exp(jax.random.uniform(key_list[4], (LEVEL_CAP, HEADS), jnp.float32, math.log(0.3), math.log(3.0))), 0.3, 3.0),
        "skip_gain": jnp.clip(jax.random.uniform(key_list[5], (HEADS,), jnp.float32, 0.5, 1.5), 0.5, 1.5),
    }


def reference(inputs, keys_in, queries, step_sizes, level_weights, skip_gain):
    seq_rows, full_width = inputs.shape
    num_heads = step_sizes.shape[1]
    head_dim = full_width // num_heads
    state_dim = keys_in.shape[1]
    block_count = seq_rows // STRETCH
    bit_count = max(1, (block_count - 1).bit_length())
    powers = 2 ** jnp.arange(bit_count, dtype=jnp.int32)
    scales = (powers.astype(jnp.float32) * STRETCH) ** -0.5
    level_coef = level_weights[1:bit_count + 1] * scales[:, None]
    causal = lax.broadcasted_iota(jnp.int32, (STRETCH, STRETCH), 0) >= lax.broadcasted_iota(jnp.int32, (STRETCH, STRETCH), 1)
    skip_vec = jnp.repeat(skip_gain, head_dim)
    highest = lax.Precision.HIGHEST

    def step_fn(carry, blocks_in):
        running, previous = carry
        x_block, k_block, q_block, dt_block, block_id = blocks_in
        values = (x_block.astype(jnp.float32).reshape(STRETCH, num_heads, head_dim) * dt_block[:, :, None]).reshape(STRETCH, full_width).astype(jnp.bfloat16)
        bit_set = ((block_id // powers) % 2).astype(jnp.float32)
        coef = bit_set[:, None] * level_coef
        combined = jnp.einsum("jh,jnhp->nhp", coef, previous.reshape(bit_count, state_dim, num_heads, head_dim), precision=highest).reshape(state_dim, full_width)
        level_out = jnp.dot(q_block.astype(jnp.float32), combined, precision=highest)
        scores = jnp.dot(q_block, k_block.T, preferred_element_type=jnp.float32)
        scores = jnp.where(causal, scores, 0.0) * (STRETCH ** -0.5)
        intra_weights = (scores[None] * level_weights[0][:, None, None]).astype(jnp.bfloat16)
        intra_out = jnp.einsum("hts,shp->thp", intra_weights.astype(jnp.float32), values.astype(jnp.float32).reshape(STRETCH, num_heads, head_dim), precision=highest).reshape(STRETCH, full_width)
        result = (x_block.astype(jnp.float32) * skip_vec[None, :] + intra_out + level_out).astype(jnp.bfloat16)
        state = jnp.dot(k_block.T, values, preferred_element_type=jnp.float32)
        running = running + state[None]
        finished = ((block_id + 1) % powers == 0)[:, None, None]
        previous = jnp.where(finished, running, previous)
        running = jnp.where(finished, 0.0, running)
        return (running, previous), result

    zeros = jnp.zeros((bit_count, state_dim, full_width), jnp.float32)
    blocks_in = (inputs.reshape(block_count, STRETCH, full_width),
                 keys_in.reshape(block_count, STRETCH, state_dim),
                 queries.reshape(block_count, STRETCH, state_dim),
                 step_sizes.reshape(block_count, STRETCH, num_heads),
                 jnp.arange(block_count, dtype=jnp.int32))
    carry_out, results = lax.scan(step_fn, (zeros, zeros), blocks_in)
    return results.reshape(seq_rows, full_width)
```

```python
import functools

import jax
import jax.numpy as jnp
from jax import lax
from jax.experimental import pallas as pl
from jax.experimental.pallas import tpu as pltpu
from jax.sharding import PartitionSpec as P

STRETCH = 64
GROUP = 4
CHUNKS = 1
TILE = 512


def arrived(ref, sem):
    pltpu.make_async_copy(ref, ref, sem).wait()


def kernel(
    x_ref, k_ref, q_ref, dt_ref, lw_ref, sg_ref, o_ref,
    vals, state, coef, acc, lhilo,
    in_up, in_down, out_up, out_down, quarter, base,
    cross_in, cross_out, total, high, plane_in, plane_out,
    up_send, up_recv, down_send, down_recv,
    gather_send, gather_recv, spread_send, spread_recv,
    plane_send, plane_recv,
):
    tokens, full = x_ref.shape
    heads = dt_ref.shape[1]
    head_dim = full // heads
    n_state = k_ref.shape[1]
    planes = lax.axis_size("sx")
    bits_high = planes.bit_length() - 1
    part = n_state // GROUP
    piece = part // GROUP
    width = full // CHUNKS
    cell = full // planes
    my_sx = lax.axis_index("sx")
    my_z = lax.axis_index("sy")
    group = my_z // GROUP
    spot = my_z % GROUP

    barrier = pltpu.get_barrier_semaphore()

    @pl.when(spot > 0)
    def _():
        pl.semaphore_signal(barrier, inc=1, device_id={"sy": my_z - 1})

    @pl.when(spot < GROUP - 1)
    def _():
        pl.semaphore_signal(barrier, inc=1, device_id={"sy": my_z + 1})

    for d in range(1, GROUP):
        pl.semaphore_signal(barrier, inc=1, device_id={"sy": (group ^ d) * GROUP + spot})

    def greet(d, carry):
        pl.semaphore_signal(barrier, inc=1, device_id={"sx": my_sx ^ d})
        return carry

    lax.fori_loop(1, planes, greet, 0)

    first_head = lax.broadcasted_iota(jnp.int32, (heads, TILE), 0) * head_dim
    lane = lax.broadcasted_iota(jnp.int32, (heads, TILE), 1)
    tile = min(TILE, full)
    rows_lw = lw_ref.shape[0]
    row_id = lax.broadcasted_iota(jnp.int32, (rows_lw, heads), 0)
    factor = jnp.full((rows_lw, heads), STRETCH**-0.5, jnp.float32)
    for level in range(1, rows_lw - 1):
        factor = jnp.where(
            row_id == level + 1, (2.0**level * STRETCH) ** -0.5, factor
        )
    table = lw_ref[...] * factor
    exact = functools.partial(
        jnp.dot, precision=lax.Precision.HIGHEST, preferred_element_type=jnp.float32
    )

    def columns(t):
        return pl.ds(pl.multiple_of(t * tile, tile), tile)

    def spread_map(t):
        col = lane[:, :tile] + t * tile
        start = first_head[:, :tile]
        return jnp.where((col >= start) & (col < start + head_dim), 1.0, 0.0)

    def make_state(t, carry):
        cols = columns(t)
        dt = exact(dt_ref[...], spread_map(t))
        v = (x_ref[:, cols].astype(jnp.float32) * dt).astype(jnp.bfloat16)
        vals[:, cols] = v
        state[:, cols] = lax.dot_general(
            k_ref[...], v, (((0,), (0,)), ((), ())), preferred_element_type=jnp.float32
        )
        coef[0:rows_lw, cols] = exact(table, spread_map(t))
        return carry

    lax.fori_loop(0, full // tile, make_state, 0)

    friends = (
        jnp.where(spot > 0, 1, 0) + jnp.where(spot < GROUP - 1, 1, 0) + (GROUP - 1) + (planes - 1)
    )
    pl.semaphore_wait(barrier, friends)

    def chunk(c):
        return pl.ds(c * width, width)

    def rows_of(j):
        return pl.ds(j * part, part)

    def send_up(c, slot, src):
        pltpu.make_async_remote_copy(
            src_ref=src, dst_ref=in_up.at[slot, :, chunk(c)],
            send_sem=up_send.at[c, slot], recv_sem=up_recv.at[c, slot],
            device_id={"sy": my_z + 1},
        ).start()

    def send_down(c, slot, src):
        pltpu.make_async_remote_copy(
            src_ref=src, dst_ref=in_down.at[slot, :, chunk(c)],
            send_sem=down_send.at[c, slot], recv_sem=down_recv.at[c, slot],
            device_id={"sy": my_z - 1},
        ).start()

    def wait_up(c, slot):
        arrived(in_up.at[slot, :, chunk(c)], up_recv.at[c, slot])

    def wait_down(c, slot):
        arrived(in_down.at[slot, :, chunk(c)], down_recv.at[c, slot])

    def st(c, j):
        return state[rows_of(j), chunk(c)]

    def up(c, slot):
        return in_up[slot, :, chunk(c)]

    def down(c, slot):
        return in_down[slot, :, chunk(c)]

    def bs(c):
        return base[:, chunk(c)]

    def weight(row, c):
        return coef[row : row + 1, chunk(c)]

    def early_start(c):
        @pl.when(spot == 0)
        def _():
            for j in (3, 2, 1, 0):
                send_up(c, j, state.at[rows_of(j), chunk(c)])

        @pl.when(spot == 2)
        def _():
            send_up(c, 4, state.at[rows_of(3), chunk(c)])

        @pl.when(spot == 3)
        def _():
            for j in (0, 1, 2):
                send_down(c, j, state.at[rows_of(j), chunk(c)])

    def early_rest(c):
        @pl.when(spot == 0)
        def _():
            wait_down(c, 0)
            quarter[:, chunk(c)] = st(c, 0) + down(c, 0)

        @pl.when(spot == 1)
        def _():
            wait_up(c, 3)
            out_up[3, :, chunk(c)] = st(c, 3) + up(c, 3)
            send_up(c, 3, out_up.at[3, :, chunk(c)])
            wait_down(c, 0)
            out_down[0, :, chunk(c)] = st(c, 0) + down(c, 0)
            send_down(c, 0, out_down.at[0, :, chunk(c)])
            wait_up(c, 2)
            out_up[2, :, chunk(c)] = st(c, 2) + up(c, 2)
            send_up(c, 2, out_up.at[2, :, chunk(c)])
            wait_up(c, 1)
            wait_down(c, 1)
            quarter[:, chunk(c)] = st(c, 1) + up(c, 1) + down(c, 1)

        @pl.when(spot == 2)
        def _():
            wait_down(c, 0)
            out_down[0, :, chunk(c)] = st(c, 0) + down(c, 0)
            send_down(c, 0, out_down.at[0, :, chunk(c)])
            wait_up(c, 3)
            send_up(c, 3, in_up.at[3, :, chunk(c)])
            wait_down(c, 1)
            out_down[1, :, chunk(c)] = st(c, 1) + down(c, 1)
            send_down(c, 1, out_down.at[1, :, chunk(c)])
            wait_up(c, 2)
            wait_down(c, 2)
            quarter[:, chunk(c)] = st(c, 2) + up(c, 2) + down(c, 2)

        @pl.when(spot == 3)
        def _():
            wait_up(c, 4)
            wait_up(c, 3)
            quarter[:, chunk(c)] = st(c, 3) + up(c, 3) + up(c, 4)

    def gather_copy(c, d):
        other = group ^ d
        return pltpu.make_async_remote_copy(
            src_ref=quarter.at[pl.ds(pl.multiple_of(other * piece, piece), piece), chunk(c)],
            dst_ref=cross_in.at[d, :, chunk(c)],
            send_sem=gather_send.at[c, d], recv_sem=gather_recv.at[c, d],
            device_id={"sy": other * GROUP + spot},
        )

    def gather_start(c):
        for d in (2, 1, 3):
            gather_copy(c, d).start()
        cross_in[0, :, chunk(c)] = quarter[
            pl.ds(pl.multiple_of(group * piece, piece), piece), chunk(c)
        ]

    def owner_sx(c, d):
        return ((my_sx // CHUNKS) ^ d) * CHUNKS + c

    def plane_start(c):
        for d in range(1, GROUP):
            arrived(cross_in.at[d, :, chunk(c)], gather_recv.at[c, d])
        total[:, chunk(c)] = (cross_in[0, :, chunk(c)] + cross_in[1, :, chunk(c)]) + (
            cross_in[2, :, chunk(c)] + cross_in[3, :, chunk(c)]
        )

        def cell_of(sx):
            start = c * width + (sx // CHUNKS) * cell
            return pl.ds(pl.multiple_of(start, cell), cell)

        def go(d, carry):
            sx = owner_sx(c, d)

            @pl.when(sx != my_sx)
            def _():
                pltpu.make_async_remote_copy(
                    src_ref=total.at[:, cell_of(sx)], dst_ref=plane_in.at[my_sx],
                    send_sem=plane_send.at[c, 0], recv_sem=plane_recv.at[c, 0],
                    device_id={"sx": sx},
                ).start()

            return carry

        lax.fori_loop(0, planes // CHUNKS, go, 0)

        @pl.when(my_sx % CHUNKS == c)
        def _():
            plane_in[my_sx] = total[:, cell_of(my_sx)]

    def plane_own(c):
        @pl.when(my_sx % CHUNKS == c)
        def _():
            mine = pl.ds(
                pl.multiple_of(c * width + (my_sx // CHUNKS) * cell, cell), cell
            )
            everyone = plane_in.at[pl.ds(0, planes - 1)]
            arrived(everyone, plane_recv.at[c, 0])
            nodes = [[plane_in[s] for s in range(planes)]]
            for level in range(bits_high - 1):
                below = nodes[-1]
                nodes.append([below[2 * n] + below[2 * n + 1] for n in range(len(below) // 2)])
            found = [jnp.zeros((piece, cell), jnp.float32)]
            for level in reversed(range(bits_high)):
                scale = coef[6 + level : 7 + level, mine]
                grown = []
                for n, upper in enumerate(found):
                    grown += [upper, upper + scale * nodes[level][2 * n]]
                found = grown
            for s in range(planes):
                plane_out[s] = found[s]

            def back(d, carry):
                sx = my_sx ^ d
                pltpu.make_async_remote_copy(
                    src_ref=plane_out.at[sx], dst_ref=high.at[:, mine],
                    send_sem=plane_send.at[c, 1], recv_sem=plane_recv.at[c, 1],
                    device_id={"sx": sx},
                ).start()
                return carry

            lax.fori_loop(1, planes, back, 0)
            high[:, mine] = plane_out[my_sx]
            arrived(plane_out.at[pl.ds(0, planes - 1)], plane_send.at[c, 1])

    def spread_copy(c, d):
        return pltpu.make_async_remote_copy(
            src_ref=cross_out.at[d, :, chunk(c)],
            dst_ref=base.at[pl.ds(pl.multiple_of(group * piece, piece), piece), chunk(c)],
            send_sem=spread_send.at[c, d], recv_sem=spread_recv.at[c, d],
            device_id={"sy": (group ^ d) * GROUP + spot},
        )

    def count_cells(c):
        return planes // CHUNKS - jnp.where(my_sx % CHUNKS == c, 1, 0)

    def wait_cells(ref, c, sem):
        cells = planes // CHUNKS

        @pl.when(my_sx % CHUNKS == c)
        def _():
            arrived(ref.at[:, pl.ds(0, (cells - 1) * cell)], sem)

        @pl.when(my_sx % CHUNKS != c)
        def _():
            arrived(ref.at[:, pl.ds(0, cells * cell)], sem)

    def spread_start(c):
        wait_cells(high, c, plane_recv.at[c, 1])
        wait_cells(total, c, plane_send.at[c, 0])
        own = high[:, chunk(c)]
        sums = [cross_in[group ^ g, :, chunk(c)] for g in range(GROUP - 1)]
        w2, w3 = weight(4, c), weight(5, c)
        pair = w3 * (sums[0] + sums[1])
        results = [own, own + w2 * sums[0], own + pair, own + pair + w2 * sums[2]]
        for g in range(GROUP):
            cross_out[group ^ g, :, chunk(c)] = results[g]
        for d in (2, 1, 3):
            spread_copy(c, d).start()
        base[pl.ds(pl.multiple_of(group * piece, piece), piece), chunk(c)] = cross_out[
            0, :, chunk(c)
        ]

    def put(c, j, value):
        high_part = value.astype(jnp.bfloat16)
        low_part = (value - high_part.astype(jnp.float32)).astype(jnp.bfloat16)
        lhilo[rows_of(j), chunk(c)] = high_part
        lhilo[pl.ds(n_state + j * part, part), chunk(c)] = low_part

    def late(c):
        for d in range(1, GROUP):
            other = group ^ d
            arrived(
                base.at[pl.ds(pl.multiple_of(other * piece, piece), piece), chunk(c)],
                spread_recv.at[c, d],
            )
        w0, w1 = weight(2, c), weight(3, c)
        mine = base.at[:, chunk(c)]

        @pl.when(spot == 0)
        def _():
            send_up(c, 4, mine)
            put(c, 0, bs(c))
            for j in (1, 2, 3):
                wait_down(c, j)
                put(c, j, down(c, j))

        @pl.when(spot == 1)
        def _():
            send_down(c, 1, mine)
            out_up[1, :, chunk(c)] = bs(c) + w1 * (st(c, 1) + up(c, 1))
            send_up(c, 1, out_up.at[1, :, chunk(c)])
            put(c, 1, bs(c) + w0 * up(c, 1))
            wait_down(c, 2)
            send_down(c, 2, in_down.at[2, :, chunk(c)])
            wait_up(c, 0)
            wait_up(c, 4)
            out_up[0, :, chunk(c)] = up(c, 4) + w1 * (st(c, 0) + up(c, 0))
            send_up(c, 0, out_up.at[0, :, chunk(c)])
            put(c, 2, down(c, 2) + w0 * up(c, 2))
            put(c, 0, up(c, 4) + w0 * up(c, 0))
            wait_down(c, 3)
            send_down(c, 3, in_down.at[3, :, chunk(c)])
            put(c, 3, down(c, 3) + w0 * up(c, 3))

        @pl.when(spot == 2)
        def _():
            send_down(c, 2, mine)
            level = bs(c) + w1 * up(c, 2)
            out_up[2, :, chunk(c)] = level + w0 * st(c, 2)
            send_up(c, 2, out_up.at[2, :, chunk(c)])
            put(c, 2, level)
            wait_down(c, 3)
            send_down(c, 3, in_down.at[3, :, chunk(c)])
            wait_up(c, 1)
            out_up[1, :, chunk(c)] = up(c, 1) + w0 * st(c, 1)
            send_up(c, 1, out_up.at[1, :, chunk(c)])
            put(c, 1, up(c, 1))
            put(c, 3, down(c, 3) + w1 * up(c, 3))
            wait_up(c, 0)
            out_up[0, :, chunk(c)] = up(c, 0) + w0 * st(c, 0)
            send_up(c, 0, out_up.at[0, :, chunk(c)])
            put(c, 0, up(c, 0))

        @pl.when(spot == 3)
        def _():
            send_down(c, 3, mine)
            put(c, 3, bs(c) + w1 * up(c, 3) + w0 * up(c, 4))
            for j in (2, 1, 0):
                wait_up(c, j)
                put(c, j, up(c, j))

    def local_part():
        scores = lax.dot_general(
            q_ref[...], k_ref[...], (((1,), (1,)), ((), ())), preferred_element_type=jnp.float32
        )
        t_id = lax.broadcasted_iota(jnp.int32, (tokens, tokens), 0)
        s_id = lax.broadcasted_iota(jnp.int32, (tokens, tokens), 1)
        same = (t_id // STRETCH) == (s_id // STRETCH)
        inside = jnp.where(same & (t_id >= s_id), scores, 0.0).astype(jnp.bfloat16)
        before = jnp.where(t_id // STRETCH > s_id // STRETCH, scores, 0.0).astype(jnp.bfloat16)
        gain = jnp.broadcast_to(sg_ref[...], (8, heads))

        def body(t, carry):
            cols = columns(t)
            v = vals[:, cols]
            skip = exact(gain, spread_map(t))[0:1]
            acc[:, cols] = (
                x_ref[:, cols].astype(jnp.float32) * skip
                + coef[0:1, cols] * jnp.dot(inside, v, preferred_element_type=jnp.float32)
                + coef[1:2, cols] * jnp.dot(before, v, preferred_element_type=jnp.float32)
            )
            return carry

        lax.fori_loop(0, full // tile, body, 0)

    def finish():
        q_twice = jnp.concatenate([q_ref[...], q_ref[...]], axis=1)

        def body(t, carry):
            cols = columns(t)
            o_ref[:, cols] = (
                acc[:, cols]
                + jnp.dot(q_twice, lhilo[:, cols], preferred_element_type=jnp.float32)
            ).astype(o_ref.dtype)
            return carry

        lax.fori_loop(0, full // tile, body, 0)

    for c in range(CHUNKS):
        early_start(c)
    local_part()
    for c in range(CHUNKS):
        early_rest(c)
        gather_start(c)
    for c in range(CHUNKS):
        plane_start(c)
    for c in range(CHUNKS):
        plane_own(c)
    for c in range(CHUNKS):
        spread_start(c)
    for c in range(CHUNKS):
        late(c)
    finish()

    for c in range(CHUNKS):
        for d in range(1, GROUP):
            gather_copy(c, d).wait_send()
            spread_copy(c, d).wait_send()

        @pl.when(spot < GROUP - 1)
        def _():
            for slot in range(4):
                arrived(in_up.at[slot, :, chunk(c)], up_send.at[c, slot])

        @pl.when((spot == 0) | (spot == 2))
        def _():
            arrived(in_up.at[4, :, chunk(c)], up_send.at[c, 4])

        @pl.when(spot > 0)
        def _():
            for slot in range(4):
                arrived(in_down.at[slot, :, chunk(c)], down_send.at[c, slot])


def on_device(inputs, keys_in, queries, step_sizes, level_weights, skip_gain):
    tokens, full = inputs.shape
    n_state = keys_in.shape[1]
    planes = lax.axis_size("sx")
    part = n_state // GROUP
    piece = part // GROUP
    f32 = jnp.float32
    vmem = pl.BlockSpec(memory_space=pltpu.VMEM)
    dma = pltpu.SemaphoreType.DMA
    return pl.pallas_call(
        kernel,
        out_shape=jax.ShapeDtypeStruct((tokens, full), jnp.bfloat16),
        in_specs=[vmem] * 6,
        out_specs=vmem,
        scratch_shapes=[
            pltpu.VMEM((tokens, full), jnp.bfloat16),
            pltpu.VMEM((n_state, full), f32),
            pltpu.VMEM((24, full), f32),
            pltpu.VMEM((tokens, full), f32),
            pltpu.VMEM((2 * n_state, full), jnp.bfloat16),
            pltpu.VMEM((5, part, full), f32),
            pltpu.VMEM((4, part, full), f32),
            pltpu.VMEM((4, part, full), f32),
            pltpu.VMEM((2, part, full), f32),
            pltpu.VMEM((part, full), f32),
            pltpu.VMEM((part, full), f32),
            pltpu.VMEM((4, piece, full), f32),
            pltpu.VMEM((4, piece, full), f32),
            pltpu.VMEM((piece, full), f32),
            pltpu.VMEM((piece, full), f32),
            pltpu.VMEM((planes, piece, full // planes), f32),
            pltpu.VMEM((planes, piece, full // planes), f32),
            dma((CHUNKS, 5)), dma((CHUNKS, 5)), dma((CHUNKS, 4)), dma((CHUNKS, 4)),
            dma((CHUNKS, 4)), dma((CHUNKS, 4)), dma((CHUNKS, 4)), dma((CHUNKS, 4)),
            dma((CHUNKS, 2)), dma((CHUNKS, 2)),
        ],
        compiler_params=pltpu.CompilerParams(
            collective_id=0, has_side_effects=True, vmem_limit_bytes=48 * 2**20
        ),
        cost_estimate=pl.CostEstimate(
            flops=10 * tokens * n_state * full, bytes_accessed=4 * tokens * full, transcendentals=0
        ),
    )(inputs, keys_in, queries, step_sizes, level_weights, skip_gain.reshape(1, -1))


def solution(mesh):
    placed = (
        P(("sx", "sy"), None),
        P(("sx", "sy"), None),
        P(("sx", "sy"), None),
        P(("sx", "sy"), None),
        P(),
        P(),
    )
    return jax.shard_map(
        on_device, mesh=mesh, in_specs=placed, out_specs=P(("sx", "sy"), None), check_vma=False
    )
```

```python
import functools

import jax
import jax.numpy as jnp
from jax import lax
from jax.experimental import pallas as pl
from jax.experimental.pallas import tpu as pltpu
from jax.sharding import PartitionSpec as P

STRETCH = 64
GROUP = 4
PIECES = 16
HALF = 8
LEAD = 2
TILE = 512
SUM_UP = (14, 12, 10, 8, 15, 13, 11, 9)
SUM_DOWN = (0, 2, 4, 6, 1, 3, 5, 7)
BACK_UP = (6, 4, 2, 0, 7, 5, 3, 1)
BACK_DOWN = (8, 10, 12, 14, 9, 11, 13, 15)


def arrived(ref, sem):
    pltpu.make_async_copy(ref, ref, sem).wait()


def kernel(
    x_ref, k_ref, q_ref, dt_ref, lw_ref, sg_ref, o_ref,
    vals, state, coef, acc, level,
    in_up, in_down, out_up, out_down, base,
    cross_in, cross_out, total, high, plane_in, plane_out,
    up_send, up_recv, down_send, down_recv,
    cross_send, cross_recv, base_recv, plane_send, plane_recv,
):
    tokens, full = x_ref.shape
    heads = dt_ref.shape[1]
    head_dim = full // heads
    n_state = k_ref.shape[1]
    planes = lax.axis_size("sx")
    bits_high = planes.bit_length() - 1
    rows = n_state // PIECES
    cell = full // planes
    tile = min(TILE, full)
    my_sx = lax.axis_index("sx")
    my_z = lax.axis_index("sy")
    group = my_z // GROUP
    spot = my_z % GROUP

    def chip(groups_on, where):
        return {"sy": (group + groups_on) % GROUP * GROUP + where}

    barrier = pltpu.get_barrier_semaphore()

    @pl.when(spot > 0)
    def _():
        pl.semaphore_signal(barrier, inc=1, device_id={"sy": my_z - 1})

    @pl.when(spot < GROUP - 1)
    def _():
        pl.semaphore_signal(barrier, inc=1, device_id={"sy": my_z + 1})

    @pl.when(spot == 0)
    def _():
        for peer in ((2, 3), (3, 0), (3, 3), (1, 0)):
            pl.semaphore_signal(barrier, inc=1, device_id=chip(*peer))

    @pl.when(spot == 3)
    def _():
        for peer in ((2, 0), (1, 3), (1, 0), (3, 3)):
            pl.semaphore_signal(barrier, inc=1, device_id=chip(*peer))

    @pl.when((spot == 0) | (spot == 3))
    def _():
        def greet(d, carry):
            pl.semaphore_signal(barrier, inc=1, device_id={"sx": my_sx ^ d})
            return carry

        lax.fori_loop(1, planes, greet, 0)

    def product(a, b, dims=((1,), (0,))):
        return lax.dot_general(a, b, (dims, ((), ())), preferred_element_type=jnp.float32)

    def columns(t):
        return pl.ds(pl.multiple_of(t * tile, tile), tile)

    shift = (group * (n_state // GROUP) + 5 * n_state // 8) % n_state
    from_id = lax.broadcasted_iota(jnp.int32, (n_state, n_state), 0)
    to_id = lax.broadcasted_iota(jnp.int32, (n_state, n_state), 1)
    turn = jnp.where(from_id == (to_id + shift) % n_state, 1.0, 0.0).astype(jnp.bfloat16)
    k_turned = product(k_ref[...], turn).astype(jnp.bfloat16)

    rows_lw = lw_ref.shape[0]
    row_id = lax.broadcasted_iota(jnp.int32, (rows_lw, heads), 0)
    factor = jnp.full((rows_lw, heads), STRETCH**-0.5, jnp.float32)
    for bit in range(1, rows_lw - 1):
        factor = jnp.where(row_id == bit + 1, (2.0**bit * STRETCH) ** -0.5, factor)
    narrow = jnp.concatenate(
        [dt_ref[...], jnp.broadcast_to(sg_ref[...], (8, heads)), lw_ref[...] * factor], axis=0
    )
    parts = []
    for _ in range(3):
        parts.append(narrow.astype(jnp.bfloat16))
        narrow = narrow - parts[-1].astype(jnp.float32)
    first_head = lax.broadcasted_iota(jnp.int32, (heads, tile), 0) * head_dim
    lane = lax.broadcasted_iota(jnp.int32, (heads, tile), 1)

    def make_state(t, carry):
        cols = columns(t)
        place = lane + t * tile - first_head
        head_map = jnp.where((place >= 0) & (place < head_dim), 1.0, 0.0).astype(jnp.bfloat16)
        wide = product(parts[0], head_map) + product(parts[1], head_map) + product(
            parts[2], head_map
        )
        v = (x_ref[:, cols].astype(jnp.float32) * wide[:tokens]).astype(jnp.bfloat16)
        vals[:, cols] = v
        state[:, cols] = product(k_turned, v, ((0,), (0,)))
        coef[0 : 8 + rows_lw, cols] = wide[tokens:]
        return carry

    lax.fori_loop(0, full // tile, make_state, 0)

    ends = jnp.where((spot == 0) | (spot == 3), 1, 0)
    pl.semaphore_wait(barrier, 2 + ends * (3 + planes - 1))

    def at(p):
        return pl.ds(p * rows, rows)

    def send_up(slot, src):
        pltpu.make_async_remote_copy(
            src_ref=src, dst_ref=in_up.at[slot], send_sem=up_send, recv_sem=up_recv.at[slot],
            device_id={"sy": my_z + 1},
        ).start()

    def send_down(slot, src):
        pltpu.make_async_remote_copy(
            src_ref=src, dst_ref=in_down.at[slot], send_sem=down_send,
            recv_sem=down_recv.at[slot], device_id={"sy": my_z - 1},
        ).start()

    def get_up(slot):
        arrived(in_up.at[slot], up_recv.at[slot])
        return in_up[slot]

    def get_down(slot):
        arrived(in_down.at[slot], down_recv.at[slot])
        return in_down[slot]

    def weight(bit):
        return coef[9 + bit : 10 + bit, :]

    def local_part():
        scores = product(q_ref[...], k_ref[...], ((1,), (1,)))
        t_id = lax.broadcasted_iota(jnp.int32, (tokens, tokens), 0)
        s_id = lax.broadcasted_iota(jnp.int32, (tokens, tokens), 1)
        same = (t_id // STRETCH) == (s_id // STRETCH)
        inside = jnp.where(same & (t_id >= s_id), scores, 0.0).astype(jnp.bfloat16)
        before = jnp.where(t_id // STRETCH > s_id // STRETCH, scores, 0.0).astype(jnp.bfloat16)

        def body(t, carry):
            cols = columns(t)
            v = vals[:, cols]
            acc[:, cols] = (
                x_ref[:, cols].astype(jnp.float32) * coef[0:1, cols]
                + coef[8:9, cols] * product(inside, v)
                + coef[9:10, cols] * product(before, v)
            )
            return carry

        lax.fori_loop(0, full // tile, body, 0)

    def group_sum(p, value):
        half = p % 2
        kind = p // 2
        targets = {
            0: (2, 3, 2), 1: (3, 0, 1), 2: (3, 3, 1),
            5: (1, 0, 3), 6: (1, 3, 3), 7: (2, 0, 2),
        }
        if kind in (3, 4):
            cross_in[half, 0] = value
            return
        groups_on, where, slot = targets[kind]
        out_up[p] = value
        pltpu.make_async_remote_copy(
            src_ref=out_up.at[p], dst_ref=cross_in.at[half, slot],
            send_sem=cross_send, recv_sem=cross_recv.at[half, slot],
            device_id=chip(groups_on, where),
        ).start()

    def cell_of(sx):
        return pl.ds(pl.multiple_of(sx * cell, cell), cell)

    def plane_start(half):
        for slot in range(1, GROUP):
            arrived(cross_in.at[half, slot], cross_recv.at[half, slot])
        total[half] = (cross_in[half, 0] + cross_in[half, 1]) + (
            cross_in[half, 2] + cross_in[half, 3]
        )

        def go(d, carry):
            sx = my_sx ^ d
            pltpu.make_async_remote_copy(
                src_ref=total.at[half, :, cell_of(sx)], dst_ref=plane_in.at[half, my_sx],
                send_sem=plane_send.at[half, 0], recv_sem=plane_recv.at[half, 0],
                device_id={"sx": sx},
            ).start()
            return carry

        lax.fori_loop(1, planes, go, 0)
        plane_in[half, my_sx] = total[half, :, cell_of(my_sx)]

    def plane_own(half):
        mine = cell_of(my_sx)
        arrived(plane_in.at[half, pl.ds(0, planes - 1)], plane_recv.at[half, 0])
        nodes = [[plane_in[half, s] for s in range(planes)]]
        for _ in range(bits_high - 1):
            below = nodes[-1]
            nodes.append([below[2 * n] + below[2 * n + 1] for n in range(len(below) // 2)])
        found = [jnp.zeros((rows, cell), jnp.float32)]
        for bit in reversed(range(bits_high)):
            scale = coef[14 + bit : 15 + bit, mine]
            grown = []
            for n, upper in enumerate(found):
                grown += [upper, upper + scale * nodes[bit][2 * n]]
            found = grown
        for s in range(planes):
            plane_out[half, s] = found[s]

        def back(d, carry):
            sx = my_sx ^ d
            pltpu.make_async_remote_copy(
                src_ref=plane_out.at[half, sx], dst_ref=high.at[half, :, mine],
                send_sem=plane_send.at[half, 1], recv_sem=plane_recv.at[half, 1],
                device_id={"sx": sx},
            ).start()
            return carry

        lax.fori_loop(1, planes, back, 0)
        high[half, :, mine] = plane_out[half, my_sx]

    def spread(half, owner):
        arrived(high.at[half, :, pl.ds(0, (planes - 1) * cell)], plane_recv.at[half, 1])
        own = high[half]
        sums = [cross_in[half, (g - group + GROUP) % GROUP] for g in range(GROUP - 1)]
        w2, w3 = weight(2 + 1), weight(3 + 1)
        pair = w3 * (sums[0] + sums[1])
        results = [own, own + w2 * sums[0], own + pair, own + pair + w2 * sums[2]]
        for g in range(GROUP):
            cross_out[half, (g - group + GROUP) % GROUP] = results[g]
        if owner == 0:
            plan = ((2, 3, 14), (1, 0, 2), (3, 3, 10), (0, 0, 6))
        else:
            plan = ((2, 0, 0), (3, 3, 12), (1, 0, 4), (0, 3, 8))
        for groups_on, where, p in plan:
            slot = (p + half) % HALF
            if groups_on == 0:
                base[slot] = cross_out[half, 0]
            else:
                pltpu.make_async_remote_copy(
                    src_ref=cross_out.at[half, groups_on], dst_ref=base.at[slot],
                    send_sem=cross_send, recv_sem=base_recv.at[slot],
                    device_id=chip(groups_on, where),
                ).start()

    def get_base(p):
        slot = p % HALF
        if p // 2 not in (3, 4):
            arrived(base.at[slot], base_recv.at[slot])
        return base[slot]

    def put(p, value):
        level[at(p), :] = value

    def end_chip(owner, sums, sum_step, later, backs, back_step):
        for p in sums[:6]:
            sum_step(p)
        plane_start(0)
        for p in sums[6:]:
            sum_step(p)
        later(0)
        plane_own(0)
        spread(0, owner)
        plane_start(1)
        for p in backs[:2]:
            back_step(p)
        plane_own(1)
        for p in backs[2:4]:
            back_step(p)
        later(1)
        spread(1, owner)
        for p in backs[4:]:
            back_step(p)

    def in_turn(first, second, lead):
        count = len(first)
        for n in range(count + lead):
            if n < count:
                first[n]()
            if n >= lead:
                second[n - lead]()

    @pl.when(spot == 0)
    def _():
        for p in SUM_UP:
            send_up(p, state.at[at(p)])
        local_part()

        def sum_step(p):
            group_sum(p, state[at(p), :] + get_down(p))

        def later(half):
            for p in BACK_UP[4 * half : 4 * half + 4]:
                send_up(p, state.at[at(p)])

        def back_step(p):
            value = get_base(p)
            send_up(PIECES + p % HALF, base.at[p % HALF])
            put(p, value)

        end_chip(0, SUM_DOWN, sum_step, later, BACK_UP, back_step)
        for r in BACK_DOWN:
            put(r, get_down(r))

    @pl.when(spot == 3)
    def _():
        for p in SUM_DOWN:
            send_down(p, state.at[at(p)])
        local_part()

        def sum_step(p):
            group_sum(p, state[at(p), :] + get_up(p))

        def back_step(r):
            value = get_base(r)
            send_down(r, base.at[r % HALF])
            put(r, value + get_up(PIECES + r % HALF))

        end_chip(3, SUM_UP, sum_step, lambda half: None, BACK_DOWN, back_step)
        for p in BACK_UP:
            put(p, get_up(p))

    w0, w1 = weight(1), weight(2)

    def each(step, order):
        return [functools.partial(step, p) for p in order]

    def sum_up(r):
        out_up[r] = state[at(r), :] + get_up(r)
        send_up(r, out_up.at[r])

    def sum_down(p):
        out_down[p] = state[at(p), :] + get_down(p)
        send_down(p, out_down.at[p])

    @pl.when(spot == 1)
    def _():
        in_turn(each(sum_up, SUM_UP), each(sum_down, SUM_DOWN), LEAD)
        local_part()

        def back_up(p):
            below = get_up(p)
            value = get_up(PIECES + p)
            out_up[p] = value + w1 * (state[at(p), :] + below)
            send_up(p, out_up.at[p])
            put(p, value + w0 * below)

        def back_down(r):
            value = get_down(r)
            send_down(r, in_down.at[r])
            put(r, value + w0 * in_up[r])

        in_turn(each(back_up, BACK_UP), each(back_down, BACK_DOWN), LEAD)

    @pl.when(spot == 2)
    def _():
        in_turn(each(sum_down, SUM_DOWN), each(sum_up, SUM_UP), LEAD)
        for r in BACK_DOWN:
            out_up[HALF + r] = w1 * in_up[r] + w0 * state[at(r), :]
            send_up(HALF + r, out_up.at[HALF + r])
        local_part()

        def back_down(r):
            value = get_down(r)
            send_down(r, in_down.at[r])
            put(r, value + w1 * in_up[r])

        def back_up(p):
            value = get_up(p)
            out_up[p] = value + w0 * state[at(p), :]
            send_up(p, out_up.at[p])
            put(p, value)

        in_turn(each(back_down, BACK_DOWN), each(back_up, BACK_UP), LEAD)

    q_turned = product(q_ref[...], turn).astype(jnp.bfloat16)

    def finish(t, carry):
        cols = columns(t)
        found = level[:, cols]
        high_part = found.astype(jnp.bfloat16)
        low_part = (found - high_part.astype(jnp.float32)).astype(jnp.bfloat16)
        o_ref[:, cols] = (
            acc[:, cols] + product(q_turned, high_part) + product(q_turned, low_part)
        ).astype(o_ref.dtype)
        return carry

    lax.fori_loop(0, full // tile, finish, 0)

    @pl.when((spot == 0) | (spot == 2))
    def _():
        arrived(in_up, up_send)

    @pl.when(spot == 1)
    def _():
        arrived(in_up.at[pl.ds(0, PIECES)], up_send)

    @pl.when(spot > 0)
    def _():
        arrived(in_down, down_send)

    @pl.when((spot == 0) | (spot == 3))
    def _():
        arrived(in_up.at[pl.ds(0, 12)], cross_send)
        for half in range(2):
            for way in range(2):
                arrived(plane_in.at[half, pl.ds(0, planes - 1)], plane_send.at[half, way])


def on_device(inputs, keys_in, queries, step_sizes, level_weights, skip_gain):
    tokens, full = inputs.shape
    n_state = keys_in.shape[1]
    planes = lax.axis_size("sx")
    rows = n_state // PIECES
    f32 = jnp.float32
    vmem = pl.BlockSpec(memory_space=pltpu.VMEM)
    dma = pltpu.SemaphoreType.DMA
    return pl.pallas_call(
        kernel,
        out_shape=jax.ShapeDtypeStruct((tokens, full), jnp.bfloat16),
        in_specs=[vmem] * 6,
        out_specs=vmem,
        scratch_shapes=[
            pltpu.VMEM((tokens, full), jnp.bfloat16),
            pltpu.VMEM((n_state, full), f32),
            pltpu.VMEM((32, full), f32),
            pltpu.VMEM((tokens, full), f32),
            pltpu.VMEM((n_state, full), f32),
            pltpu.VMEM((PIECES + HALF, rows, full), f32),
            pltpu.VMEM((PIECES, rows, full), f32),
            pltpu.VMEM((PIECES + HALF, rows, full), f32),
            pltpu.VMEM((HALF, rows, full), f32),
            pltpu.VMEM((HALF, rows, full), f32),
            pltpu.VMEM((2, GROUP, rows, full), f32),
            pltpu.VMEM((2, GROUP, rows, full), f32),
            pltpu.VMEM((2, rows, full), f32),
            pltpu.VMEM((2, rows, full), f32),
            pltpu.VMEM((2, planes, rows, full // planes), f32),
            pltpu.VMEM((2, planes, rows, full // planes), f32),
            dma, dma((PIECES + HALF,)), dma, dma((PIECES,)),
            dma, dma((2, GROUP)), dma((HALF,)), dma((2, 2)), dma((2, 2)),
        ],
        compiler_params=pltpu.CompilerParams(
            collective_id=0, has_side_effects=True, vmem_limit_bytes=48 * 2**20
        ),
        cost_estimate=pl.CostEstimate(
            flops=10 * tokens * n_state * full, bytes_accessed=4 * tokens * full, transcendentals=0
        ),
    )(inputs, keys_in, queries, step_sizes, level_weights, skip_gain.reshape(1, -1))


def solution(mesh):
    placed = (
        P(("sx", "sy"), None),
        P(("sx", "sy"), None),
        P(("sx", "sy"), None),
        P(("sx", "sy"), None),
        P(),
        P(),
    )
    return jax.shard_map(
        on_device, mesh=mesh, in_specs=placed, out_specs=P(("sx", "sy"), None), check_vma=False
    )
```

```python
import functools

import jax
import jax.numpy as jnp
from jax import lax
from jax.experimental import pallas as pl
from jax.experimental.pallas import tpu as pltpu
from jax.sharding import PartitionSpec as P

STRETCH = 64
GROUP = 4
PIECES = 16
HALF = 8
LEAD = 2
TILE = 512
SUM_UP = (14, 12, 10, 8, 15, 13, 11, 9)
SUM_DOWN = (0, 2, 4, 6, 1, 3, 5, 7)
BACK_UP = (6, 4, 2, 0, 7, 5, 3, 1)
BACK_DOWN = (8, 10, 12, 14, 9, 11, 13, 15)


def arrived(ref, sem):
    pltpu.make_async_copy(ref, ref, sem).wait()


def kernel(
    x_ref, k_ref, q_ref, dt_ref, lw_ref, sg_ref, o_ref,
    vals, state, coef, acc, level,
    in_up, in_down, out_up, out_down, base,
    cross_in, cross_out, total, high, plane_in, plane_out,
    up_send, up_recv, down_send, down_recv,
    cross_send, cross_recv, base_recv, plane_send, plane_recv,
):
    tokens, full = x_ref.shape
    heads = dt_ref.shape[1]
    head_dim = full // heads
    n_state = k_ref.shape[1]
    planes = lax.axis_size("sx")
    bits_high = planes.bit_length() - 1
    rows = n_state // PIECES
    cell = full // planes
    tile = min(TILE, full)
    my_sx = lax.axis_index("sx")
    my_z = lax.axis_index("sy")
    group = my_z // GROUP
    spot = my_z % GROUP

    def chip(groups_on, where):
        return {"sy": (group + groups_on) % GROUP * GROUP + where}

    barrier = pltpu.get_barrier_semaphore()

    @pl.when(spot > 0)
    def _():
        pl.semaphore_signal(barrier, inc=1, device_id={"sy": my_z - 1})

    @pl.when(spot < GROUP - 1)
    def _():
        pl.semaphore_signal(barrier, inc=1, device_id={"sy": my_z + 1})

    @pl.when(spot == 0)
    def _():
        for peer in ((2, 3), (3, 0), (3, 3), (1, 0)):
            pl.semaphore_signal(barrier, inc=1, device_id=chip(*peer))

    @pl.when(spot == 3)
    def _():
        for peer in ((2, 0), (1, 3), (1, 0), (3, 3)):
            pl.semaphore_signal(barrier, inc=1, device_id=chip(*peer))

    @pl.when((spot == 0) | (spot == 3))
    def _():
        def greet(d, carry):
            pl.semaphore_signal(barrier, inc=1, device_id={"sx": my_sx ^ d})
            return carry

        lax.fori_loop(1, planes, greet, 0)

    def product(a, b, dims=((1,), (0,))):
        return lax.dot_general(a, b, (dims, ((), ())), preferred_element_type=jnp.float32)

    def columns(t):
        return pl.ds(pl.multiple_of(t * tile, tile), tile)

    shift = (group * (n_state // GROUP) + 5 * n_state // 8) % n_state
    from_id = lax.broadcasted_iota(jnp.int32, (n_state, n_state), 0)
    to_id = lax.broadcasted_iota(jnp.int32, (n_state, n_state), 1)
    turn = jnp.where(from_id == (to_id + shift) % n_state, 1.0, 0.0).astype(jnp.bfloat16)
    k_turned = product(k_ref[...], turn).astype(jnp.bfloat16)

    rows_lw = lw_ref.shape[0]
    row_id = lax.broadcasted_iota(jnp.int32, (rows_lw, heads), 0)
    factor = jnp.full((rows_lw, heads), STRETCH**-0.5, jnp.float32)
    for bit in range(1, rows_lw - 1):
        factor = jnp.where(row_id == bit + 1, (2.0**bit * STRETCH) ** -0.5, factor)
    narrow = jnp.concatenate(
        [dt_ref[...], jnp.broadcast_to(sg_ref[...], (8, heads)), lw_ref[...] * factor], axis=0
    )
    parts = []
    for _ in range(3):
        parts.append(narrow.astype(jnp.bfloat16))
        narrow = narrow - parts[-1].astype(jnp.float32)
    first_head = lax.broadcasted_iota(jnp.int32, (heads, tile), 0) * head_dim
    lane = lax.broadcasted_iota(jnp.int32, (heads, tile), 1)

    def make_state(t, carry):
        cols = columns(t)
        place = lane + t * tile - first_head
        head_map = jnp.where((place >= 0) & (place < head_dim), 1.0, 0.0).astype(jnp.bfloat16)
        wide = product(parts[0], head_map) + product(parts[1], head_map) + product(
            parts[2], head_map
        )
        v = (x_ref[:, cols].astype(jnp.float32) * wide[:tokens]).astype(jnp.bfloat16)
        vals[:, cols] = v
        state[:, cols] = product(k_turned, v, ((0,), (0,)))
        coef[0 : 8 + rows_lw, cols] = wide[tokens:]
        return carry

    lax.fori_loop(0, full // tile, make_state, 0)

    ends = jnp.where((spot == 0) | (spot == 3), 1, 0)
    pl.semaphore_wait(barrier, 2 + ends * (3 + planes - 1))

    def at(p):
        return pl.ds(p * rows, rows)

    def send_up(slot, src):
        pltpu.make_async_remote_copy(
            src_ref=src, dst_ref=in_up.at[slot], send_sem=up_send, recv_sem=up_recv.at[slot],
            device_id={"sy": my_z + 1},
        ).start()

    def send_down(slot, src):
        pltpu.make_async_remote_copy(
            src_ref=src, dst_ref=in_down.at[slot], send_sem=down_send,
            recv_sem=down_recv.at[slot], device_id={"sy": my_z - 1},
        ).start()

    def get_up(slot):
        arrived(in_up.at[slot], up_recv.at[slot])
        return in_up[slot]

    def get_down(slot):
        arrived(in_down.at[slot], down_recv.at[slot])
        return in_down[slot]

    def weight(bit):
        return coef[9 + bit : 10 + bit, :]

    def local_part():
        scores = product(q_ref[...], k_ref[...], ((1,), (1,)))
        t_id = lax.broadcasted_iota(jnp.int32, (tokens, tokens), 0)
        s_id = lax.broadcasted_iota(jnp.int32, (tokens, tokens), 1)
        same = (t_id // STRETCH) == (s_id // STRETCH)
        inside = jnp.where(same & (t_id >= s_id), scores, 0.0).astype(jnp.bfloat16)
        before = jnp.where(t_id // STRETCH > s_id // STRETCH, scores, 0.0).astype(jnp.bfloat16)

        def body(t, carry):
            cols = columns(t)
            v = vals[:, cols]
            acc[:, cols] = (
                x_ref[:, cols].astype(jnp.float32) * coef[0:1, cols]
                + coef[8:9, cols] * product(inside, v)
                + coef[9:10, cols] * product(before, v)
            )
            return carry

        lax.fori_loop(0, full // tile, body, 0)

    def group_sum(p, value):
        half = p % 2
        kind = p // 2
        targets = {
            0: (2, 3, 2), 1: (3, 0, 1), 2: (3, 3, 1),
            5: (1, 0, 3), 6: (1, 3, 3), 7: (2, 0, 2),
        }
        if kind in (3, 4):
            cross_in[half, 0] = value
            return
        groups_on, where, slot = targets[kind]
        out_up[p] = value
        pltpu.make_async_remote_copy(
            src_ref=out_up.at[p], dst_ref=cross_in.at[half, slot],
            send_sem=cross_send, recv_sem=cross_recv.at[half, slot],
            device_id=chip(groups_on, where),
        ).start()

    def cell_of(sx):
        return pl.ds(pl.multiple_of(sx * cell, cell), cell)

    def plane_start(half):
        for slot in range(1, GROUP):
            arrived(cross_in.at[half, slot], cross_recv.at[half, slot])
        total[half] = (cross_in[half, 0] + cross_in[half, 1]) + (
            cross_in[half, 2] + cross_in[half, 3]
        )

        def go(d, carry):
            sx = my_sx ^ d
            pltpu.make_async_remote_copy(
                src_ref=total.at[half, :, cell_of(sx)], dst_ref=plane_in.at[half, my_sx],
                send_sem=plane_send.at[half, 0], recv_sem=plane_recv.at[half, 0],
                device_id={"sx": sx},
            ).start()
            return carry

        lax.fori_loop(1, planes, go, 0)
        plane_in[half, my_sx] = total[half, :, cell_of(my_sx)]

    def plane_own(half):
        mine = cell_of(my_sx)
        arrived(plane_in.at[half, pl.ds(0, planes - 1)], plane_recv.at[half, 0])
        nodes = [[plane_in[half, s] for s in range(planes)]]
        for _ in range(bits_high - 1):
            below = nodes[-1]
            nodes.append([below[2 * n] + below[2 * n + 1] for n in range(len(below) // 2)])
        found = [jnp.zeros((rows, cell), jnp.float32)]
        for bit in reversed(range(bits_high)):
            scale = coef[14 + bit : 15 + bit, mine]
            grown = []
            for n, upper in enumerate(found):
                grown += [upper, upper + scale * nodes[bit][2 * n]]
            found = grown
        for s in range(planes):
            plane_out[half, s] = found[s]

        def back(d, carry):
            sx = my_sx ^ d
            pltpu.make_async_remote_copy(
                src_ref=plane_out.at[half, sx], dst_ref=high.at[half, :, mine],
                send_sem=plane_send.at[half, 1], recv_sem=plane_recv.at[half, 1],
                device_id={"sx": sx},
            ).start()
            return carry

        lax.fori_loop(1, planes, back, 0)
        high[half, :, mine] = plane_out[half, my_sx]

    def spread(half, owner):
        arrived(high.at[half, :, pl.ds(0, (planes - 1) * cell)], plane_recv.at[half, 1])
        own = high[half]
        sums = [cross_in[half, (g - group + GROUP) % GROUP] for g in range(GROUP - 1)]
        w2, w3 = weight(2 + 1), weight(3 + 1)
        pair = w3 * (sums[0] + sums[1])
        results = [own, own + w2 * sums[0], own + pair, own + pair + w2 * sums[2]]
        for g in range(GROUP):
            cross_out[half, (g - group + GROUP) % GROUP] = results[g]
        if owner == 0:
            plan = ((2, 3, 14), (1, 0, 2), (3, 3, 10), (0, 0, 6))
        else:
            plan = ((2, 0, 0), (3, 3, 12), (1, 0, 4), (0, 3, 8))
        for groups_on, where, p in plan:
            slot = (p + half) % HALF
            if groups_on == 0:
                base[slot] = cross_out[half, 0]
            else:
                pltpu.make_async_remote_copy(
                    src_ref=cross_out.at[half, groups_on], dst_ref=base.at[slot],
                    send_sem=cross_send, recv_sem=base_recv.at[slot],
                    device_id=chip(groups_on, where),
                ).start()

    def get_base(p):
        slot = p % HALF
        if p // 2 not in (3, 4):
            arrived(base.at[slot], base_recv.at[slot])
        return base[slot]

    def put(p, value):
        level[at(p), :] = value

    def end_chip(owner, sums, sum_step, later, backs, back_step):
        for p in sums[:6]:
            sum_step(p)
        plane_start(0)
        for p in sums[6:]:
            sum_step(p)
        plane_own(0)
        spread(0, owner)
        plane_start(1)
        for p in backs[:2]:
            back_step(p)
        plane_own(1)
        for p in backs[2:4]:
            back_step(p)
        spread(1, owner)
        for p in backs[4:]:
            back_step(p)

    def in_turn(first, second, lead):
        count = len(first)
        for n in range(count + lead):
            if n < count:
                first[n]()
            if n >= lead:
                second[n - lead]()

    @pl.when(spot == 0)
    def _():
        for p in SUM_UP:
            send_up(p, state.at[at(p)])
        for p in BACK_UP:
            send_up(p, state.at[at(p)])
        local_part()

        def sum_step(p):
            group_sum(p, state[at(p), :] + get_down(p))

        def later(half):
            for p in BACK_UP[4 * half : 4 * half + 4]:
                send_up(p, state.at[at(p)])

        def back_step(p):
            value = get_base(p)
            send_up(PIECES + p % HALF, base.at[p % HALF])
            put(p, value)

        end_chip(0, SUM_DOWN, sum_step, later, BACK_UP, back_step)
        for r in BACK_DOWN:
            put(r, get_down(r))

    @pl.when(spot == 3)
    def _():
        for p in SUM_DOWN:
            send_down(p, state.at[at(p)])
        local_part()

        def sum_step(p):
            group_sum(p, state[at(p), :] + get_up(p))

        def back_step(r):
            value = get_base(r)
            send_down(r, base.at[r % HALF])
            put(r, value + get_up(PIECES + r % HALF))

        end_chip(3, SUM_UP, sum_step, lambda half: None, BACK_DOWN, back_step)
        for p in BACK_UP:
            put(p, get_up(p))

    w0, w1 = weight(1), weight(2)

    def each(step, order):
        return [functools.partial(step, p) for p in order]

    def sum_up(r):
        out_up[r] = state[at(r), :] + get_up(r)
        send_up(r, out_up.at[r])

    def sum_down(p):
        out_down[p] = state[at(p), :] + get_down(p)
        send_down(p, out_down.at[p])

    @pl.when(spot == 1)
    def _():
        in_turn(each(sum_up, SUM_UP), each(sum_down, SUM_DOWN), LEAD)
        local_part()

        def back_up(p):
            below = get_up(p)
            value = get_up(PIECES + p)
            out_up[p] = value + w1 * (state[at(p), :] + below)
            send_up(p, out_up.at[p])
            put(p, value + w0 * below)

        def back_down(r):
            value = get_down(r)
            send_down(r, in_down.at[r])
            put(r, value + w0 * in_up[r])

        in_turn(each(back_up, BACK_UP), each(back_down, BACK_DOWN), LEAD)

    @pl.when(spot == 2)
    def _():
        in_turn(each(sum_down, SUM_DOWN), each(sum_up, SUM_UP), LEAD)
        for r in BACK_DOWN:
            out_up[HALF + r] = w1 * in_up[r] + w0 * state[at(r), :]
            send_up(HALF + r, out_up.at[HALF + r])
        local_part()

        def back_down(r):
            value = get_down(r)
            send_down(r, in_down.at[r])
            put(r, value + w1 * in_up[r])

        def back_up(p):
            value = get_up(p)
            out_up[p] = value + w0 * state[at(p), :]
            send_up(p, out_up.at[p])
            put(p, value)

        in_turn(each(back_down, BACK_DOWN), each(back_up, BACK_UP), LEAD)

    q_turned = product(q_ref[...], turn).astype(jnp.bfloat16)

    def finish(t, carry):
        cols = columns(t)
        found = level[:, cols]
        high_part = found.astype(jnp.bfloat16)
        low_part = (found - high_part.astype(jnp.float32)).astype(jnp.bfloat16)
        o_ref[:, cols] = (
            acc[:, cols] + product(q_turned, high_part) + product(q_turned, low_part)
        ).astype(o_ref.dtype)
        return carry

    lax.fori_loop(0, full // tile, finish, 0)

    @pl.when((spot == 0) | (spot == 2))
    def _():
        arrived(in_up, up_send)

    @pl.when(spot == 1)
    def _():
        arrived(in_up.at[pl.ds(0, PIECES)], up_send)

    @pl.when(spot > 0)
    def _():
        arrived(in_down, down_send)

    @pl.when((spot == 0) | (spot == 3))
    def _():
        arrived(in_up.at[pl.ds(0, 12)], cross_send)
        for half in range(2):
            for way in range(2):
                arrived(plane_in.at[half, pl.ds(0, planes - 1)], plane_send.at[half, way])


def on_device(inputs, keys_in, queries, step_sizes, level_weights, skip_gain):
    tokens, full = inputs.shape
    n_state = keys_in.shape[1]
    planes = lax.axis_size("sx")
    rows = n_state // PIECES
    f32 = jnp.float32
    vmem = pl.BlockSpec(memory_space=pltpu.VMEM)
    dma = pltpu.SemaphoreType.DMA
    return pl.pallas_call(
        kernel,
        out_shape=jax.ShapeDtypeStruct((tokens, full), jnp.bfloat16),
        in_specs=[vmem] * 6,
        out_specs=vmem,
        scratch_shapes=[
            pltpu.VMEM((tokens, full), jnp.bfloat16),
            pltpu.VMEM((n_state, full), f32),
            pltpu.VMEM((32, full), f32),
            pltpu.VMEM((tokens, full), f32),
            pltpu.VMEM((n_state, full), f32),
            pltpu.VMEM((PIECES + HALF, rows, full), f32),
            pltpu.VMEM((PIECES, rows, full), f32),
            pltpu.VMEM((PIECES + HALF, rows, full), f32),
            pltpu.VMEM((HALF, rows, full), f32),
            pltpu.VMEM((HALF, rows, full), f32),
            pltpu.VMEM((2, GROUP, rows, full), f32),
            pltpu.VMEM((2, GROUP, rows, full), f32),
            pltpu.VMEM((2, rows, full), f32),
            pltpu.VMEM((2, rows, full), f32),
            pltpu.VMEM((2, planes, rows, full // planes), f32),
            pltpu.VMEM((2, planes, rows, full // planes), f32),
            dma, dma((PIECES + HALF,)), dma, dma((PIECES,)),
            dma, dma((2, GROUP)), dma((HALF,)), dma((2, 2)), dma((2, 2)),
        ],
        compiler_params=pltpu.CompilerParams(
            collective_id=0, has_side_effects=True, vmem_limit_bytes=48 * 2**20
        ),
        cost_estimate=pl.CostEstimate(
            flops=10 * tokens * n_state * full, bytes_accessed=4 * tokens * full, transcendentals=0
        ),
    )(inputs, keys_in, queries, step_sizes, level_weights, skip_gain.reshape(1, -1))


def solution(mesh):
    placed = (
        P(("sx", "sy"), None),
        P(("sx", "sy"), None),
        P(("sx", "sy"), None),
        P(("sx", "sy"), None),
        P(),
        P(),
    )
    return jax.shard_map(
        on_device, mesh=mesh, in_specs=placed, out_specs=P(("sx", "sy"), None), check_vma=False
    )
```

```python
import functools

import jax
import jax.numpy as jnp
from jax import lax
from jax.experimental import pallas as pl
from jax.experimental.pallas import tpu as pltpu
from jax.sharding import PartitionSpec as P

STRETCH = 64
GROUP = 4
PIECES = 16
HALF = 8
LEAD = 1
TILE = 512
SUM_UP = (14, 12, 10, 8, 15, 13, 11, 9)
SUM_DOWN = (0, 2, 4, 6, 1, 3, 5, 7)
BACK_UP = (6, 4, 2, 0, 7, 5, 3, 1)
BACK_DOWN = (8, 10, 12, 14, 9, 11, 13, 15)


def arrived(ref, sem):
    pltpu.make_async_copy(ref, ref, sem).wait()


def kernel(
    x_ref, k_ref, q_ref, dt_ref, lw_ref, sg_ref, o_ref,
    vals, state, coef, acc, level,
    in_up, in_down, out_up, out_down, base,
    cross_in, cross_out, total, high, plane_in, plane_out,
    up_send, up_recv, down_send, down_recv,
    cross_send, cross_recv, base_recv, plane_send, plane_recv,
):
    tokens, full = x_ref.shape
    heads = dt_ref.shape[1]
    head_dim = full // heads
    n_state = k_ref.shape[1]
    planes = lax.axis_size("sx")
    bits_high = planes.bit_length() - 1
    rows = n_state // PIECES
    cell = full // planes
    tile = min(TILE, full)
    my_sx = lax.axis_index("sx")
    my_z = lax.axis_index("sy")
    group = my_z // GROUP
    spot = my_z % GROUP

    def chip(groups_on, where):
        return {"sy": (group + groups_on) % GROUP * GROUP + where}

    barrier = pltpu.get_barrier_semaphore()

    @pl.when(spot > 0)
    def _():
        pl.semaphore_signal(barrier, inc=1, device_id={"sy": my_z - 1})

    @pl.when(spot < GROUP - 1)
    def _():
        pl.semaphore_signal(barrier, inc=1, device_id={"sy": my_z + 1})

    @pl.when(spot == 0)
    def _():
        for peer in ((2, 3), (3, 0), (3, 3), (1, 0)):
            pl.semaphore_signal(barrier, inc=1, device_id=chip(*peer))

    @pl.when(spot == 3)
    def _():
        for peer in ((2, 0), (1, 3), (1, 0), (3, 3)):
            pl.semaphore_signal(barrier, inc=1, device_id=chip(*peer))

    @pl.when((spot == 0) | (spot == 3))
    def _():
        def greet(d, carry):
            pl.semaphore_signal(barrier, inc=1, device_id={"sx": my_sx ^ d})
            return carry

        lax.fori_loop(1, planes, greet, 0)

    def product(a, b, dims=((1,), (0,))):
        return lax.dot_general(a, b, (dims, ((), ())), preferred_element_type=jnp.float32)

    def columns(t):
        return pl.ds(pl.multiple_of(t * tile, tile), tile)

    shift = (group * (n_state // GROUP) + 5 * n_state // 8) % n_state
    from_id = lax.broadcasted_iota(jnp.int32, (n_state, n_state), 0)
    to_id = lax.broadcasted_iota(jnp.int32, (n_state, n_state), 1)
    turn = jnp.where(from_id == (to_id + shift) % n_state, 1.0, 0.0).astype(jnp.bfloat16)
    k_turned = product(k_ref[...], turn).astype(jnp.bfloat16)

    rows_lw = lw_ref.shape[0]
    row_id = lax.broadcasted_iota(jnp.int32, (rows_lw, heads), 0)
    factor = jnp.full((rows_lw, heads), STRETCH**-0.5, jnp.float32)
    for bit in range(1, rows_lw - 1):
        factor = jnp.where(row_id == bit + 1, (2.0**bit * STRETCH) ** -0.5, factor)
    narrow = jnp.concatenate(
        [dt_ref[...], jnp.broadcast_to(sg_ref[...], (8, heads)), lw_ref[...] * factor], axis=0
    )
    parts = []
    for _ in range(3):
        parts.append(narrow.astype(jnp.bfloat16))
        narrow = narrow - parts[-1].astype(jnp.float32)
    first_head = lax.broadcasted_iota(jnp.int32, (heads, tile), 0) * head_dim
    lane = lax.broadcasted_iota(jnp.int32, (heads, tile), 1)

    def make_state(t, carry):
        cols = columns(t)
        place = lane + t * tile - first_head
        head_map = jnp.where((place >= 0) & (place < head_dim), 1.0, 0.0).astype(jnp.bfloat16)
        wide = product(parts[0], head_map) + product(parts[1], head_map) + product(
            parts[2], head_map
        )
        v = (x_ref[:, cols].astype(jnp.float32) * wide[:tokens]).astype(jnp.bfloat16)
        vals[:, cols] = v
        state[:, cols] = product(k_turned, v, ((0,), (0,)))
        coef[0 : 8 + rows_lw, cols] = wide[tokens:]
        return carry

    lax.fori_loop(0, full // tile, make_state, 0)

    ends = jnp.where((spot == 0) | (spot == 3), 1, 0)
    pl.semaphore_wait(barrier, 2 + ends * (3 + planes - 1))

    def at(p):
        return pl.ds(p * rows, rows)

    def send_up(slot, src):
        pltpu.make_async_remote_copy(
            src_ref=src, dst_ref=in_up.at[slot], send_sem=up_send, recv_sem=up_recv.at[slot],
            device_id={"sy": my_z + 1},
        ).start()

    def send_down(slot, src):
        pltpu.make_async_remote_copy(
            src_ref=src, dst_ref=in_down.at[slot], send_sem=down_send,
            recv_sem=down_recv.at[slot], device_id={"sy": my_z - 1},
        ).start()

    def get_up(slot):
        arrived(in_up.at[slot], up_recv.at[slot])
        return in_up[slot]

    def get_down(slot):
        arrived(in_down.at[slot], down_recv.at[slot])
        return in_down[slot]

    def weight(bit):
        return coef[9 + bit : 10 + bit, :]

    def local_part():
        scores = product(q_ref[...], k_ref[...], ((1,), (1,)))
        t_id = lax.broadcasted_iota(jnp.int32, (tokens, tokens), 0)
        s_id = lax.broadcasted_iota(jnp.int32, (tokens, tokens), 1)
        same = (t_id // STRETCH) == (s_id // STRETCH)
        inside = jnp.where(same & (t_id >= s_id), scores, 0.0).astype(jnp.bfloat16)
        before = jnp.where(t_id // STRETCH > s_id // STRETCH, scores, 0.0).astype(jnp.bfloat16)

        def body(t, carry):
            cols = columns(t)
            v = vals[:, cols]
            acc[:, cols] = (
                x_ref[:, cols].astype(jnp.float32) * coef[0:1, cols]
                + coef[8:9, cols] * product(inside, v)
                + coef[9:10, cols] * product(before, v)
            )
            return carry

        lax.fori_loop(0, full // tile, body, 0)

    def group_sum(p, value):
        half = p % 2
        kind = p // 2
        targets = {
            0: (2, 3, 2), 1: (3, 0, 1), 2: (3, 3, 1),
            5: (1, 0, 3), 6: (1, 3, 3), 7: (2, 0, 2),
        }
        if kind in (3, 4):
            cross_in[half, 0] = value
            return
        groups_on, where, slot = targets[kind]
        out_up[p] = value
        pltpu.make_async_remote_copy(
            src_ref=out_up.at[p], dst_ref=cross_in.at[half, slot],
            send_sem=cross_send, recv_sem=cross_recv.at[half, slot],
            device_id=chip(groups_on, where),
        ).start()

    def cell_of(sx):
        return pl.ds(pl.multiple_of(sx * cell, cell), cell)

    def plane_start(half):
        for slot in range(1, GROUP):
            arrived(cross_in.at[half, slot], cross_recv.at[half, slot])
        total[half] = (cross_in[half, 0] + cross_in[half, 1]) + (
            cross_in[half, 2] + cross_in[half, 3]
        )

        def go(d, carry):
            sx = my_sx ^ d
            pltpu.make_async_remote_copy(
                src_ref=total.at[half, :, cell_of(sx)], dst_ref=plane_in.at[half, my_sx],
                send_sem=plane_send.at[half, 0], recv_sem=plane_recv.at[half, 0],
                device_id={"sx": sx},
            ).start()
            return carry

        lax.fori_loop(1, planes, go, 0)
        plane_in[half, my_sx] = total[half, :, cell_of(my_sx)]

    def plane_own(half):
        mine = cell_of(my_sx)
        arrived(plane_in.at[half, pl.ds(0, planes - 1)], plane_recv.at[half, 0])
        nodes = [[plane_in[half, s] for s in range(planes)]]
        for _ in range(bits_high - 1):
            below = nodes[-1]
            nodes.append([below[2 * n] + below[2 * n + 1] for n in range(len(below) // 2)])
        found = [jnp.zeros((rows, cell), jnp.float32)]
        for bit in reversed(range(bits_high)):
            scale = coef[14 + bit : 15 + bit, mine]
            grown = []
            for n, upper in enumerate(found):
                grown += [upper, upper + scale * nodes[bit][2 * n]]
            found = grown
        for s in range(planes):
            plane_out[half, s] = found[s]

        def back(d, carry):
            sx = my_sx ^ d
            pltpu.make_async_remote_copy(
                src_ref=plane_out.at[half, sx], dst_ref=high.at[half, :, mine],
                send_sem=plane_send.at[half, 1], recv_sem=plane_recv.at[half, 1],
                device_id={"sx": sx},
            ).start()
            return carry

        lax.fori_loop(1, planes, back, 0)
        high[half, :, mine] = plane_out[half, my_sx]

    def spread(half, owner):
        arrived(high.at[half, :, pl.ds(0, (planes - 1) * cell)], plane_recv.at[half, 1])
        own = high[half]
        sums = [cross_in[half, (g - group + GROUP) % GROUP] for g in range(GROUP - 1)]
        w2, w3 = weight(2 + 1), weight(3 + 1)
        pair = w3 * (sums[0] + sums[1])
        results = [own, own + w2 * sums[0], own + pair, own + pair + w2 * sums[2]]
        for g in range(GROUP):
            cross_out[half, (g - group + GROUP) % GROUP] = results[g]
        if owner == 0:
            plan = ((2, 3, 14), (1, 0, 2), (3, 3, 10), (0, 0, 6))
        else:
            plan = ((2, 0, 0), (3, 3, 12), (1, 0, 4), (0, 3, 8))
        for groups_on, where, p in plan:
            slot = (p + half) % HALF
            if groups_on == 0:
                base[slot] = cross_out[half, 0]
            else:
                pltpu.make_async_remote_copy(
                    src_ref=cross_out.at[half, groups_on], dst_ref=base.at[slot],
                    send_sem=cross_send, recv_sem=base_recv.at[slot],
                    device_id=chip(groups_on, where),
                ).start()

    def get_base(p):
        slot = p % HALF
        if p // 2 not in (3, 4):
            arrived(base.at[slot], base_recv.at[slot])
        return base[slot]

    def put(p, value):
        level[at(p), :] = value

    def end_chip(owner, sums, sum_step, backs, back_step):
        for p in sums[:6]:
            sum_step(p)
        plane_start(0)
        for p in sums[6:]:
            sum_step(p)
        plane_own(0)
        spread(0, owner)
        plane_start(1)
        plane_own(1)
        for p in backs[:4]:
            back_step(p)
        spread(1, owner)
        for p in backs[4:]:
            back_step(p)

    def in_turn(first, second, lead):
        count = len(first)
        for n in range(count + lead):
            if n < count:
                first[n]()
            if n >= lead:
                second[n - lead]()

    @pl.when(spot == 0)
    def _():
        for p in SUM_UP + BACK_UP:
            send_up(p, state.at[at(p)])
        local_part()

        def sum_step(p):
            group_sum(p, state[at(p), :] + get_down(p))

        def back_step(p):
            value = get_base(p)
            send_up(PIECES + p % HALF, base.at[p % HALF])
            put(p, value)

        end_chip(0, SUM_DOWN, sum_step, BACK_UP, back_step)
        for r in BACK_DOWN:
            put(r, get_down(r))

    @pl.when(spot == 3)
    def _():
        for p in SUM_DOWN:
            send_down(p, state.at[at(p)])
        local_part()

        def sum_step(p):
            group_sum(p, state[at(p), :] + get_up(p))

        def back_step(r):
            get_base(r)
            send_down(r, base.at[r % HALF])

        end_chip(3, SUM_UP, sum_step, BACK_DOWN, back_step)
        for p, r in zip(BACK_UP, BACK_DOWN):
            put(r, base[r % HALF] + get_up(PIECES + r % HALF))
            put(p, get_up(p))

    w0, w1 = weight(1), weight(2)

    def each(step, order):
        return [functools.partial(step, p) for p in order]

    def sum_up(r):
        out_up[r] = state[at(r), :] + get_up(r)
        send_up(r, out_up.at[r])

    def sum_down(p):
        out_down[p] = state[at(p), :] + get_down(p)
        send_down(p, out_down.at[p])

    @pl.when(spot == 1)
    def _():
        in_turn(each(sum_up, SUM_UP), each(sum_down, SUM_DOWN), LEAD)
        local_part()

        def back_up(p):
            below = get_up(p)
            value = get_up(PIECES + p)
            out_up[p] = value + w1 * (state[at(p), :] + below)
            send_up(p, out_up.at[p])
            put(p, value + w0 * below)

        def back_down(r):
            value = get_down(r)
            send_down(r, in_down.at[r])
            put(r, value + w0 * in_up[r])

        in_turn(each(back_up, BACK_UP), each(back_down, BACK_DOWN), LEAD)

    @pl.when(spot == 2)
    def _():
        in_turn(each(sum_down, SUM_DOWN), each(sum_up, SUM_UP), LEAD)
        for r in BACK_DOWN:
            out_up[HALF + r] = w1 * in_up[r] + w0 * state[at(r), :]
            send_up(HALF + r, out_up.at[HALF + r])
        local_part()

        def back_down(r):
            value = get_down(r)
            send_down(r, in_down.at[r])
            put(r, value + w1 * in_up[r])

        def back_up(p):
            value = get_up(p)
            out_up[p] = value + w0 * state[at(p), :]
            send_up(p, out_up.at[p])
            put(p, value)

        in_turn(each(back_down, BACK_DOWN), each(back_up, BACK_UP), LEAD)

    q_turned = product(q_ref[...], turn).astype(jnp.bfloat16)

    def finish(t, carry):
        cols = columns(t)
        found = level[:, cols]
        high_part = found.astype(jnp.bfloat16)
        low_part = (found - high_part.astype(jnp.float32)).astype(jnp.bfloat16)
        o_ref[:, cols] = (
            acc[:, cols] + product(q_turned, high_part) + product(q_turned, low_part)
        ).astype(o_ref.dtype)
        return carry

    lax.fori_loop(0, full // tile, finish, 0)

    @pl.when((spot == 0) | (spot == 2))
    def _():
        arrived(in_up, up_send)

    @pl.when(spot == 1)
    def _():
        arrived(in_up.at[pl.ds(0, PIECES)], up_send)

    @pl.when(spot > 0)
    def _():
        arrived(in_down, down_send)

    @pl.when((spot == 0) | (spot == 3))
    def _():
        arrived(in_up.at[pl.ds(0, 12)], cross_send)
        for half in range(2):
            for way in range(2):
                arrived(plane_in.at[half, pl.ds(0, planes - 1)], plane_send.at[half, way])


def on_device(inputs, keys_in, queries, step_sizes, level_weights, skip_gain):
    tokens, full = inputs.shape
    n_state = keys_in.shape[1]
    planes = lax.axis_size("sx")
    rows = n_state // PIECES
    f32 = jnp.float32
    vmem = pl.BlockSpec(memory_space=pltpu.VMEM)
    dma = pltpu.SemaphoreType.DMA
    return pl.pallas_call(
        kernel,
        out_shape=jax.ShapeDtypeStruct((tokens, full), jnp.bfloat16),
        in_specs=[vmem] * 6,
        out_specs=vmem,
        scratch_shapes=[
            pltpu.VMEM((tokens, full), jnp.bfloat16),
            pltpu.VMEM((n_state, full), f32),
            pltpu.VMEM((32, full), f32),
            pltpu.VMEM((tokens, full), f32),
            pltpu.VMEM((n_state, full), f32),
            pltpu.VMEM((PIECES + HALF, rows, full), f32),
            pltpu.VMEM((PIECES, rows, full), f32),
            pltpu.VMEM((PIECES + HALF, rows, full), f32),
            pltpu.VMEM((HALF, rows, full), f32),
            pltpu.VMEM((HALF, rows, full), f32),
            pltpu.VMEM((2, GROUP, rows, full), f32),
            pltpu.VMEM((2, GROUP, rows, full), f32),
            pltpu.VMEM((2, rows, full), f32),
            pltpu.VMEM((2, rows, full), f32),
            pltpu.VMEM((2, planes, rows, full // planes), f32),
            pltpu.VMEM((2, planes, rows, full // planes), f32),
            dma, dma((PIECES + HALF,)), dma, dma((PIECES,)),
            dma, dma((2, GROUP)), dma((HALF,)), dma((2, 2)), dma((2, 2)),
        ],
        compiler_params=pltpu.CompilerParams(
            collective_id=0, has_side_effects=True, vmem_limit_bytes=48 * 2**20
        ),
        cost_estimate=pl.CostEstimate(
            flops=10 * tokens * n_state * full, bytes_accessed=4 * tokens * full, transcendentals=0
        ),
    )(inputs, keys_in, queries, step_sizes, level_weights, skip_gain.reshape(1, -1))


def solution(mesh):
    placed = (
        P(("sx", "sy"), None),
        P(("sx", "sy"), None),
        P(("sx", "sy"), None),
        P(("sx", "sy"), None),
        P(),
        P(),
    )
    return jax.shard_map(
        on_device, mesh=mesh, in_specs=placed, out_specs=P(("sx", "sy"), None), check_vma=False
    )
```

```python
import functools

import jax
import jax.numpy as jnp
from jax import lax
from jax.experimental import pallas as pl
from jax.experimental.pallas import tpu as pltpu
from jax.sharding import PartitionSpec as P

STRETCH = 64
GROUP = 4
PIECES = 16
HALF = 8
LEAD = 1
TILE = 512
SUM_UP = (14, 12, 10, 8, 15, 13, 11, 9)
SUM_DOWN = (0, 2, 4, 6, 1, 3, 5, 7)
BACK_UP = (6, 4, 2, 0, 7, 5, 3, 1)
BACK_DOWN = (8, 10, 12, 14, 9, 11, 13, 15)


def arrived(ref, sem):
    pltpu.make_async_copy(ref, ref, sem).wait()


def kernel(
    x_ref, k_ref, q_ref, dt_ref, lw_ref, sg_ref, o_ref,
    vals, state, coef, acc, level,
    in_up, in_down, out_up, out_down, base,
    cross_in, cross_out, total, high, plane_in, plane_out,
    up_send, up_recv, down_send, down_recv,
    cross_send, cross_recv, base_recv, plane_send, plane_recv,
):
    tokens, full = x_ref.shape
    heads = dt_ref.shape[1]
    head_dim = full // heads
    n_state = k_ref.shape[1]
    planes = lax.axis_size("sx")
    bits_high = planes.bit_length() - 1
    rows = n_state // PIECES
    cell = full // planes
    tile = min(TILE, full)
    my_sx = lax.axis_index("sx")
    my_z = lax.axis_index("sy")
    group = my_z // GROUP
    spot = my_z % GROUP

    def chip(groups_on, where):
        return {"sy": (group + groups_on) % GROUP * GROUP + where}

    barrier = pltpu.get_barrier_semaphore()

    @pl.when(spot > 0)
    def _():
        pl.semaphore_signal(barrier, inc=1, device_id={"sy": my_z - 1})

    @pl.when(spot < GROUP - 1)
    def _():
        pl.semaphore_signal(barrier, inc=1, device_id={"sy": my_z + 1})

    @pl.when(spot == 0)
    def _():
        for peer in ((2, 3), (3, 0), (3, 3), (1, 0)):
            pl.semaphore_signal(barrier, inc=1, device_id=chip(*peer))

    @pl.when(spot == 3)
    def _():
        for peer in ((2, 0), (1, 3), (1, 0), (3, 3)):
            pl.semaphore_signal(barrier, inc=1, device_id=chip(*peer))

    @pl.when((spot == 0) | (spot == 3))
    def _():
        def greet(d, carry):
            pl.semaphore_signal(barrier, inc=1, device_id={"sx": my_sx ^ d})
            return carry

        lax.fori_loop(1, planes, greet, 0)

    def product(a, b, dims=((1,), (0,))):
        return lax.dot_general(a, b, (dims, ((), ())), preferred_element_type=jnp.float32)

    def columns(t):
        return pl.ds(pl.multiple_of(t * tile, tile), tile)

    shift = (group * (n_state // GROUP) + 5 * n_state // 8) % n_state
    from_id = lax.broadcasted_iota(jnp.int32, (n_state, n_state), 0)
    to_id = lax.broadcasted_iota(jnp.int32, (n_state, n_state), 1)
    turn = jnp.where(from_id == (to_id + shift) % n_state, 1.0, 0.0).astype(jnp.bfloat16)
    k_turned = product(k_ref[...], turn).astype(jnp.bfloat16)

    rows_lw = lw_ref.shape[0]
    row_id = lax.broadcasted_iota(jnp.int32, (rows_lw, heads), 0)
    factor = jnp.full((rows_lw, heads), STRETCH**-0.5, jnp.float32)
    for bit in range(1, rows_lw - 1):
        factor = jnp.where(row_id == bit + 1, (2.0**bit * STRETCH) ** -0.5, factor)
    narrow = jnp.concatenate(
        [dt_ref[...], jnp.broadcast_to(sg_ref[...], (8, heads)), lw_ref[...] * factor], axis=0
    )
    parts = []
    for _ in range(3):
        parts.append(narrow.astype(jnp.bfloat16))
        narrow = narrow - parts[-1].astype(jnp.float32)
    first_head = lax.broadcasted_iota(jnp.int32, (heads, tile), 0) * head_dim
    lane = lax.broadcasted_iota(jnp.int32, (heads, tile), 1)

    def make_state(t, carry):
        cols = columns(t)
        place = lane + t * tile - first_head
        head_map = jnp.where((place >= 0) & (place < head_dim), 1.0, 0.0).astype(jnp.bfloat16)
        wide = product(parts[0], head_map) + product(parts[1], head_map) + product(
            parts[2], head_map
        )
        v = (x_ref[:, cols].astype(jnp.float32) * wide[:tokens]).astype(jnp.bfloat16)
        vals[:, cols] = v
        state[:, cols] = product(k_turned, v, ((0,), (0,)))
        coef[0 : 8 + rows_lw, cols] = wide[tokens:]
        return carry

    lax.fori_loop(0, full // tile, make_state, 0)

    ends = jnp.where((spot == 0) | (spot == 3), 1, 0)
    pl.semaphore_wait(barrier, 2 + ends * (3 + planes - 1))

    def at(p):
        return pl.ds(p * rows, rows)

    def send_up(slot, src):
        pltpu.make_async_remote_copy(
            src_ref=src, dst_ref=in_up.at[slot], send_sem=up_send, recv_sem=up_recv.at[slot],
            device_id={"sy": my_z + 1},
        ).start()

    def send_down(slot, src):
        pltpu.make_async_remote_copy(
            src_ref=src, dst_ref=in_down.at[slot], send_sem=down_send,
            recv_sem=down_recv.at[slot], device_id={"sy": my_z - 1},
        ).start()

    def get_up(slot):
        arrived(in_up.at[slot], up_recv.at[slot])
        return in_up[slot]

    def get_down(slot):
        arrived(in_down.at[slot], down_recv.at[slot])
        return in_down[slot]

    def weight(bit):
        return coef[9 + bit : 10 + bit, :]

    def local_part():
        scores = product(q_ref[...], k_ref[...], ((1,), (1,)))
        t_id = lax.broadcasted_iota(jnp.int32, (tokens, tokens), 0)
        s_id = lax.broadcasted_iota(jnp.int32, (tokens, tokens), 1)
        same = (t_id // STRETCH) == (s_id // STRETCH)
        inside = jnp.where(same & (t_id >= s_id), scores, 0.0).astype(jnp.bfloat16)
        before = jnp.where(t_id // STRETCH > s_id // STRETCH, scores, 0.0).astype(jnp.bfloat16)

        def body(t, carry):
            cols = columns(t)
            v = vals[:, cols]
            acc[:, cols] = (
                x_ref[:, cols].astype(jnp.float32) * coef[0:1, cols]
                + coef[8:9, cols] * product(inside, v)
                + coef[9:10, cols] * product(before, v)
            )
            return carry

        lax.fori_loop(0, full // tile, body, 0)

    def group_sum(p, value):
        half = p % 2
        kind = p // 2
        targets = {
            0: (2, 3, 2), 1: (3, 0, 1), 2: (3, 3, 1),
            5: (1, 0, 3), 6: (1, 3, 3), 7: (2, 0, 2),
        }
        if kind in (3, 4):
            cross_in[half, 0] = value
            return
        groups_on, where, slot = targets[kind]
        out_up[p] = value
        pltpu.make_async_remote_copy(
            src_ref=out_up.at[p], dst_ref=cross_in.at[half, slot],
            send_sem=cross_send, recv_sem=cross_recv.at[half, slot],
            device_id=chip(groups_on, where),
        ).start()

    def cell_of(sx):
        return pl.ds(pl.multiple_of(sx * cell, cell), cell)

    def plane_start(half):
        for slot in range(1, GROUP):
            arrived(cross_in.at[half, slot], cross_recv.at[half, slot])
        total[half] = (cross_in[half, 0] + cross_in[half, 1]) + (
            cross_in[half, 2] + cross_in[half, 3]
        )

        def go(d, carry):
            sx = my_sx ^ d
            pltpu.make_async_remote_copy(
                src_ref=total.at[half, :, cell_of(sx)], dst_ref=plane_in.at[half, my_sx],
                send_sem=plane_send.at[half, 0], recv_sem=plane_recv.at[half, 0],
                device_id={"sx": sx},
            ).start()
            return carry

        lax.fori_loop(1, planes, go, 0)
        plane_in[half, my_sx] = total[half, :, cell_of(my_sx)]

    def plane_own(half):
        mine = cell_of(my_sx)
        arrived(plane_in.at[half, pl.ds(0, planes - 1)], plane_recv.at[half, 0])
        nodes = [[plane_in[half, s] for s in range(planes)]]
        for _ in range(bits_high - 1):
            below = nodes[-1]
            nodes.append([below[2 * n] + below[2 * n + 1] for n in range(len(below) // 2)])
        found = [jnp.zeros((rows, cell), jnp.float32)]
        for bit in reversed(range(bits_high)):
            scale = coef[14 + bit : 15 + bit, mine]
            grown = []
            for n, upper in enumerate(found):
                grown += [upper, upper + scale * nodes[bit][2 * n]]
            found = grown
        for s in range(planes):
            plane_out[half, s] = found[s]

        def back(d, carry):
            sx = my_sx ^ d
            pltpu.make_async_remote_copy(
                src_ref=plane_out.at[half, sx], dst_ref=high.at[half, :, mine],
                send_sem=plane_send.at[half, 1], recv_sem=plane_recv.at[half, 1],
                device_id={"sx": sx},
            ).start()
            return carry

        lax.fori_loop(1, planes, back, 0)
        high[half, :, mine] = plane_out[half, my_sx]

    def spread(half, owner):
        arrived(high.at[half, :, pl.ds(0, (planes - 1) * cell)], plane_recv.at[half, 1])
        own = high[half]
        sums = [cross_in[half, (g - group + GROUP) % GROUP] for g in range(GROUP - 1)]
        w2, w3 = weight(2 + 1), weight(3 + 1)
        pair = w3 * (sums[0] + sums[1])
        results = [own, own + w2 * sums[0], own + pair, own + pair + w2 * sums[2]]
        for g in range(GROUP):
            cross_out[half, (g - group + GROUP) % GROUP] = results[g]
        if owner == 0:
            plan = ((2, 3, 14), (1, 0, 2), (3, 3, 10), (0, 0, 6))
        else:
            plan = ((2, 0, 0), (3, 3, 12), (1, 0, 4), (0, 3, 8))
        for groups_on, where, p in plan:
            slot = (p + half) % HALF
            if groups_on == 0:
                base[slot] = cross_out[half, 0]
            else:
                pltpu.make_async_remote_copy(
                    src_ref=cross_out.at[half, groups_on], dst_ref=base.at[slot],
                    send_sem=cross_send, recv_sem=base_recv.at[slot],
                    device_id=chip(groups_on, where),
                ).start()

    def get_base(p):
        slot = p % HALF
        if p // 2 not in (3, 4):
            arrived(base.at[slot], base_recv.at[slot])
        return base[slot]

    def put(p, value):
        level[at(p), :] = value

    def end_chip(owner, sums, sum_step, backs, back_step):
        for p in sums[:5]:
            sum_step(p)
        plane_start(0)
        for p in sums[5:]:
            sum_step(p)
        plane_own(0)
        spread(0, owner)
        plane_start(1)
        plane_own(1)
        for p in backs[:4]:
            back_step(p)
        spread(1, owner)
        for p in backs[4:]:
            back_step(p)

    def in_turn(first, second, lead):
        count = len(first)
        for n in range(count + lead):
            if n < count:
                first[n]()
            if n >= lead:
                second[n - lead]()

    @pl.when(spot == 0)
    def _():
        for p in SUM_UP + BACK_UP:
            send_up(p, state.at[at(p)])
        local_part()

        def sum_step(p):
            group_sum(p, state[at(p), :] + get_down(p))

        def back_step(p):
            value = get_base(p)
            send_up(PIECES + p % HALF, base.at[p % HALF])
            put(p, value)

        end_chip(0, SUM_DOWN, sum_step, BACK_UP, back_step)
        for r in BACK_DOWN:
            put(r, get_down(r))

    @pl.when(spot == 3)
    def _():
        for p in SUM_DOWN:
            send_down(p, state.at[at(p)])
        local_part()

        def sum_step(p):
            group_sum(p, state[at(p), :] + get_up(p))

        def back_step(r):
            get_base(r)
            send_down(r, base.at[r % HALF])

        end_chip(3, SUM_UP, sum_step, BACK_DOWN, back_step)
        for p, r in zip(BACK_UP, BACK_DOWN):
            put(r, base[r % HALF] + get_up(PIECES + r % HALF))
            put(p, get_up(p))

    w0, w1 = weight(1), weight(2)

    def each(step, order):
        return [functools.partial(step, p) for p in order]

    def sum_up(r):
        out_up[r] = state[at(r), :] + get_up(r)
        send_up(r, out_up.at[r])

    def sum_down(p):
        out_down[p] = state[at(p), :] + get_down(p)
        send_down(p, out_down.at[p])

    @pl.when(spot == 1)
    def _():
        in_turn(each(sum_up, SUM_UP), each(sum_down, SUM_DOWN), LEAD)
        local_part()

        def back_up(p):
            below = get_up(p)
            value = get_up(PIECES + p)
            out_up[p] = value + w1 * (state[at(p), :] + below)
            send_up(p, out_up.at[p])
            put(p, value + w0 * below)

        def back_down(r):
            value = get_down(r)
            send_down(r, in_down.at[r])
            put(r, value + w0 * in_up[r])

        in_turn(each(back_up, BACK_UP), each(back_down, BACK_DOWN), LEAD)

    @pl.when(spot == 2)
    def _():
        in_turn(each(sum_down, SUM_DOWN), each(sum_up, SUM_UP), LEAD)
        for r in BACK_DOWN:
            out_up[HALF + r] = w1 * in_up[r] + w0 * state[at(r), :]
            send_up(HALF + r, out_up.at[HALF + r])
        local_part()

        def back_down(r):
            value = get_down(r)
            send_down(r, in_down.at[r])
            put(r, value + w1 * in_up[r])

        def back_up(p):
            value = get_up(p)
            out_up[p] = value + w0 * state[at(p), :]
            send_up(p, out_up.at[p])
            put(p, value)

        in_turn(each(back_down, BACK_DOWN), each(back_up, BACK_UP), LEAD + 1)

    q_turned = product(q_ref[...], turn).astype(jnp.bfloat16)

    def finish(t, carry):
        cols = columns(t)
        found = level[:, cols]
        high_part = found.astype(jnp.bfloat16)
        low_part = (found - high_part.astype(jnp.float32)).astype(jnp.bfloat16)
        o_ref[:, cols] = (
            acc[:, cols] + product(q_turned, high_part) + product(q_turned, low_part)
        ).astype(o_ref.dtype)
        return carry

    lax.fori_loop(0, full // tile, finish, 0)

    @pl.when((spot == 0) | (spot == 2))
    def _():
        arrived(in_up, up_send)

    @pl.when(spot == 1)
    def _():
        arrived(in_up.at[pl.ds(0, PIECES)], up_send)

    @pl.when(spot > 0)
    def _():
        arrived(in_down, down_send)

    @pl.when((spot == 0) | (spot == 3))
    def _():
        arrived(in_up.at[pl.ds(0, 12)], cross_send)
        for half in range(2):
            for way in range(2):
                arrived(plane_in.at[half, pl.ds(0, planes - 1)], plane_send.at[half, way])


def on_device(inputs, keys_in, queries, step_sizes, level_weights, skip_gain):
    tokens, full = inputs.shape
    n_state = keys_in.shape[1]
    planes = lax.axis_size("sx")
    rows = n_state // PIECES
    f32 = jnp.float32
    vmem = pl.BlockSpec(memory_space=pltpu.VMEM)
    dma = pltpu.SemaphoreType.DMA
    return pl.pallas_call(
        kernel,
        out_shape=jax.ShapeDtypeStruct((tokens, full), jnp.bfloat16),
        in_specs=[vmem] * 6,
        out_specs=vmem,
        scratch_shapes=[
            pltpu.VMEM((tokens, full), jnp.bfloat16),
            pltpu.VMEM((n_state, full), f32),
            pltpu.VMEM((32, full), f32),
            pltpu.VMEM((tokens, full), f32),
            pltpu.VMEM((n_state, full), f32),
            pltpu.VMEM((PIECES + HALF, rows, full), f32),
            pltpu.VMEM((PIECES, rows, full), f32),
            pltpu.VMEM((PIECES + HALF, rows, full), f32),
            pltpu.VMEM((HALF, rows, full), f32),
            pltpu.VMEM((HALF, rows, full), f32),
            pltpu.VMEM((2, GROUP, rows, full), f32),
            pltpu.VMEM((2, GROUP, rows, full), f32),
            pltpu.VMEM((2, rows, full), f32),
            pltpu.VMEM((2, rows, full), f32),
            pltpu.VMEM((2, planes, rows, full // planes), f32),
            pltpu.VMEM((2, planes, rows, full // planes), f32),
            dma, dma((PIECES + HALF,)), dma, dma((PIECES,)),
            dma, dma((2, GROUP)), dma((HALF,)), dma((2, 2)), dma((2, 2)),
        ],
        compiler_params=pltpu.CompilerParams(
            collective_id=0, has_side_effects=True, vmem_limit_bytes=48 * 2**20
        ),
        cost_estimate=pl.CostEstimate(
            flops=10 * tokens * n_state * full, bytes_accessed=4 * tokens * full, transcendentals=0
        ),
    )(inputs, keys_in, queries, step_sizes, level_weights, skip_gain.reshape(1, -1))


def solution(mesh):
    placed = (
        P(("sx", "sy"), None),
        P(("sx", "sy"), None),
        P(("sx", "sy"), None),
        P(("sx", "sy"), None),
        P(),
        P(),
    )
    return jax.shard_map(
        on_device, mesh=mesh, in_specs=placed, out_specs=P(("sx", "sy"), None), check_vma=False
    )
```

```python
import functools

import jax
import jax.numpy as jnp
from jax import lax
from jax.experimental import pallas as pl
from jax.experimental.pallas import tpu as pltpu
from jax.sharding import PartitionSpec as P

STRETCH = 64
GROUP = 4
PIECES = 16
HALF = 8
LEAD = 1
TILE = 512
SUM_UP = (14, 12, 10, 8, 15, 13, 11, 9)
SUM_DOWN = (0, 2, 4, 6, 1, 3, 5, 7)
BACK_UP = (6, 4, 2, 0, 7, 5, 3, 1)
BACK_DOWN = (8, 10, 12, 14, 9, 11, 13, 15)


def arrived(ref, sem):
    pltpu.make_async_copy(ref, ref, sem).wait()


def kernel(
    x_ref, k_ref, q_ref, dt_ref, lw_ref, sg_ref, o_ref,
    vals, state, coef, acc, level,
    in_up, in_down, out_up, out_down, base,
    cross_in, cross_out, total, high, plane_in, plane_out,
    up_send, up_recv, down_send, down_recv,
    cross_send, cross_recv, base_recv, plane_send, plane_recv,
):
    tokens, full = x_ref.shape
    heads = dt_ref.shape[1]
    head_dim = full // heads
    n_state = k_ref.shape[1]
    planes = lax.axis_size("sx")
    bits_high = planes.bit_length() - 1
    rows = n_state // PIECES
    cell = full // planes
    tile = min(TILE, full)
    my_sx = lax.axis_index("sx")
    my_z = lax.axis_index("sy")
    group = my_z // GROUP
    spot = my_z % GROUP

    def chip(groups_on, where):
        return {"sy": (group + groups_on) % GROUP * GROUP + where}

    barrier = pltpu.get_barrier_semaphore()

    @pl.when(spot > 0)
    def _():
        pl.semaphore_signal(barrier, inc=1, device_id={"sy": my_z - 1})

    @pl.when(spot < GROUP - 1)
    def _():
        pl.semaphore_signal(barrier, inc=1, device_id={"sy": my_z + 1})

    @pl.when(spot == 0)
    def _():
        for peer in ((2, 3), (3, 0), (3, 3), (1, 0)):
            pl.semaphore_signal(barrier, inc=1, device_id=chip(*peer))

    @pl.when(spot == 3)
    def _():
        for peer in ((2, 0), (1, 3), (1, 0), (3, 3)):
            pl.semaphore_signal(barrier, inc=1, device_id=chip(*peer))

    @pl.when((spot == 0) | (spot == 3))
    def _():
        def greet(d, carry):
            pl.semaphore_signal(barrier, inc=1, device_id={"sx": my_sx ^ d})
            return carry

        lax.fori_loop(1, planes, greet, 0)

    def product(a, b, dims=((1,), (0,))):
        return lax.dot_general(a, b, (dims, ((), ())), preferred_element_type=jnp.float32)

    def columns(t):
        return pl.ds(pl.multiple_of(t * tile, tile), tile)

    shift = (group * (n_state // GROUP) + 5 * n_state // 8) % n_state
    from_id = lax.broadcasted_iota(jnp.int32, (n_state, n_state), 0)
    to_id = lax.broadcasted_iota(jnp.int32, (n_state, n_state), 1)
    turn = jnp.where(from_id == (to_id + shift) % n_state, 1.0, 0.0).astype(jnp.bfloat16)
    k_turned = product(k_ref[...], turn).astype(jnp.bfloat16)

    rows_lw = lw_ref.shape[0]
    row_id = lax.broadcasted_iota(jnp.int32, (rows_lw, heads), 0)
    factor = jnp.full((rows_lw, heads), STRETCH**-0.5, jnp.float32)
    for bit in range(1, rows_lw - 1):
        factor = jnp.where(row_id == bit + 1, (2.0**bit * STRETCH) ** -0.5, factor)
    narrow = jnp.concatenate(
        [dt_ref[...], jnp.broadcast_to(sg_ref[...], (8, heads)), lw_ref[...] * factor], axis=0
    )
    parts = []
    for _ in range(3):
        parts.append(narrow.astype(jnp.bfloat16))
        narrow = narrow - parts[-1].astype(jnp.float32)
    first_head = lax.broadcasted_iota(jnp.int32, (heads, tile), 0) * head_dim
    lane = lax.broadcasted_iota(jnp.int32, (heads, tile), 1)

    def make_state(t, carry):
        cols = columns(t)
        place = lane + t * tile - first_head
        head_map = jnp.where((place >= 0) & (place < head_dim), 1.0, 0.0).astype(jnp.bfloat16)
        wide = product(parts[0], head_map) + product(parts[1], head_map) + product(
            parts[2], head_map
        )
        v = (x_ref[:, cols].astype(jnp.float32) * wide[:tokens]).astype(jnp.bfloat16)
        vals[:, cols] = v
        state[:, cols] = product(k_turned, v, ((0,), (0,)))
        coef[0 : 8 + rows_lw, cols] = wide[tokens:]
        return carry

    lax.fori_loop(0, full // tile, make_state, 0)

    ends = jnp.where((spot == 0) | (spot == 3), 1, 0)
    pl.semaphore_wait(barrier, 2 + ends * (3 + planes - 1))

    def at(p):
        return pl.ds(p * rows, rows)

    def send_up(slot, src):
        pltpu.make_async_remote_copy(
            src_ref=src, dst_ref=in_up.at[slot], send_sem=up_send, recv_sem=up_recv.at[slot],
            device_id={"sy": my_z + 1},
        ).start()

    def send_down(slot, src):
        pltpu.make_async_remote_copy(
            src_ref=src, dst_ref=in_down.at[slot], send_sem=down_send,
            recv_sem=down_recv.at[slot], device_id={"sy": my_z - 1},
        ).start()

    def get_up(slot):
        arrived(in_up.at[slot], up_recv.at[slot])
        return in_up[slot]

    def get_down(slot):
        arrived(in_down.at[slot], down_recv.at[slot])
        return in_down[slot]

    def weight(bit):
        return coef[9 + bit : 10 + bit, :]

    def local_part():
        scores = product(q_ref[...], k_ref[...], ((1,), (1,)))
        t_id = lax.broadcasted_iota(jnp.int32, (tokens, tokens), 0)
        s_id = lax.broadcasted_iota(jnp.int32, (tokens, tokens), 1)
        same = (t_id // STRETCH) == (s_id // STRETCH)
        inside = jnp.where(same & (t_id >= s_id), scores, 0.0).astype(jnp.bfloat16)
        before = jnp.where(t_id // STRETCH > s_id // STRETCH, scores, 0.0).astype(jnp.bfloat16)

        def body(t, carry):
            cols = columns(t)
            v = vals[:, cols]
            acc[:, cols] = (
                x_ref[:, cols].astype(jnp.float32) * coef[0:1, cols]
                + coef[8:9, cols] * product(inside, v)
                + coef[9:10, cols] * product(before, v)
            )
            return carry

        lax.fori_loop(0, full // tile, body, 0)

    def group_sum(p, value):
        half = p % 2
        kind = p // 2
        targets = {
            0: (2, 3, 2), 1: (3, 0, 1), 2: (3, 3, 1),
            5: (1, 0, 3), 6: (1, 3, 3), 7: (2, 0, 2),
        }
        if kind in (3, 4):
            cross_in[half, 0] = value
            return
        groups_on, where, slot = targets[kind]
        out_up[p] = value
        pltpu.make_async_remote_copy(
            src_ref=out_up.at[p], dst_ref=cross_in.at[half, slot],
            send_sem=cross_send, recv_sem=cross_recv.at[half, slot],
            device_id=chip(groups_on, where),
        ).start()

    def cell_of(sx):
        return pl.ds(pl.multiple_of(sx * cell, cell), cell)

    def plane_start(half):
        for slot in range(1, GROUP):
            arrived(cross_in.at[half, slot], cross_recv.at[half, slot])
        total[half] = (cross_in[half, 0] + cross_in[half, 1]) + (
            cross_in[half, 2] + cross_in[half, 3]
        )

        def go(d, carry):
            sx = my_sx ^ d
            pltpu.make_async_remote_copy(
                src_ref=total.at[half, :, cell_of(sx)], dst_ref=plane_in.at[half, my_sx],
                send_sem=plane_send.at[half, 0], recv_sem=plane_recv.at[half, 0],
                device_id={"sx": sx},
            ).start()
            return carry

        lax.fori_loop(1, planes, go, 0)
        plane_in[half, my_sx] = total[half, :, cell_of(my_sx)]

    def plane_own(half):
        mine = cell_of(my_sx)
        arrived(plane_in.at[half, pl.ds(0, planes - 1)], plane_recv.at[half, 0])
        nodes = [[plane_in[half, s] for s in range(planes)]]
        for _ in range(bits_high - 1):
            below = nodes[-1]
            nodes.append([below[2 * n] + below[2 * n + 1] for n in range(len(below) // 2)])
        found = [jnp.zeros((rows, cell), jnp.float32)]
        for bit in reversed(range(bits_high)):
            scale = coef[14 + bit : 15 + bit, mine]
            grown = []
            for n, upper in enumerate(found):
                grown += [upper, upper + scale * nodes[bit][2 * n]]
            found = grown
        for s in range(planes):
            plane_out[half, s] = found[s]

        def back(d, carry):
            sx = my_sx ^ d
            pltpu.make_async_remote_copy(
                src_ref=plane_out.at[half, sx], dst_ref=high.at[half, :, mine],
                send_sem=plane_send.at[half, 1], recv_sem=plane_recv.at[half, 1],
                device_id={"sx": sx},
            ).start()
            return carry

        lax.fori_loop(1, planes, back, 0)
        high[half, :, mine] = plane_out[half, my_sx]

    def spread(half, owner):
        arrived(high.at[half, :, pl.ds(0, (planes - 1) * cell)], plane_recv.at[half, 1])
        own = high[half]
        sums = [cross_in[half, (g - group + GROUP) % GROUP] for g in range(GROUP - 1)]
        w2, w3 = weight(2 + 1), weight(3 + 1)
        pair = w3 * (sums[0] + sums[1])
        results = [own, own + w2 * sums[0], own + pair, own + pair + w2 * sums[2]]
        for g in range(GROUP):
            cross_out[half, (g - group + GROUP) % GROUP] = results[g]
        if owner == 0:
            plan = ((2, 3, 14), (1, 0, 2), (3, 3, 10), (0, 0, 6))
        else:
            plan = ((2, 0, 0), (3, 3, 12), (1, 0, 4), (0, 3, 8))
        for groups_on, where, p in plan:
            slot = (p + half) % HALF
            if groups_on == 0:
                base[slot] = cross_out[half, 0]
            else:
                pltpu.make_async_remote_copy(
                    src_ref=cross_out.at[half, groups_on], dst_ref=base.at[slot],
                    send_sem=cross_send, recv_sem=base_recv.at[slot],
                    device_id=chip(groups_on, where),
                ).start()

    def get_base(p):
        slot = p % HALF
        if p // 2 not in (3, 4):
            arrived(base.at[slot], base_recv.at[slot])
        return base[slot]

    def put(p, value):
        level[at(p), :] = value

    def end_chip(owner, sums, sum_step, backs, back_step):
        for p in sums[:5]:
            sum_step(p)
        plane_start(0)
        for p in sums[5:]:
            sum_step(p)
        plane_own(0)
        spread(0, owner)
        plane_start(1)
        plane_own(1)
        for p in backs[:4]:
            back_step(p)
        spread(1, owner)
        for p in backs[4:]:
            back_step(p)

    def in_turn(first, second, lead):
        count = len(first)
        for n in range(count + lead):
            if n < count:
                first[n]()
            if n >= lead:
                second[n - lead]()

    @pl.when(spot == 0)
    def _():
        for p in SUM_UP + BACK_UP:
            send_up(p, state.at[at(p)])
        local_part()

        def sum_step(p):
            group_sum(p, state[at(p), :] + get_down(p))

        def back_step(p):
            value = get_base(p)
            send_up(PIECES + p % HALF, base.at[p % HALF])
            put(p, value)

        end_chip(0, SUM_DOWN, sum_step, BACK_UP, back_step)
        for r in BACK_DOWN:
            put(r, get_down(r))

    @pl.when(spot == 3)
    def _():
        for p in SUM_DOWN:
            send_down(p, state.at[at(p)])
        local_part()

        def sum_step(p):
            group_sum(p, state[at(p), :] + get_up(p))

        def back_step(r):
            get_base(r)
            send_down(r, base.at[r % HALF])

        end_chip(3, SUM_UP, sum_step, BACK_DOWN, back_step)
        for p, r in zip(BACK_UP, BACK_DOWN):
            put(r, base[r % HALF] + get_up(PIECES + r % HALF))
            put(p, get_up(p))

    w0, w1 = weight(1), weight(2)

    def each(step, order):
        return [functools.partial(step, p) for p in order]

    def sum_up(r):
        out_up[r] = state[at(r), :] + get_up(r)
        send_up(r, out_up.at[r])

    def sum_down(p):
        out_down[p] = state[at(p), :] + get_down(p)
        send_down(p, out_down.at[p])

    @pl.when(spot == 1)
    def _():
        in_turn(each(sum_up, SUM_UP), each(sum_down, SUM_DOWN), LEAD)
        local_part()

        def back_up(p):
            below = get_up(p)
            value = get_up(PIECES + p)
            out_up[p] = value + w1 * (state[at(p), :] + below)
            send_up(p, out_up.at[p])
            put(p, value + w0 * below)

        def back_down(r):
            value = get_down(r)
            send_down(r, in_down.at[r])
            put(r, value + w0 * in_up[r])

        in_turn(each(back_up, BACK_UP), each(back_down, BACK_DOWN), LEAD)

    @pl.when(spot == 2)
    def _():
        in_turn(each(sum_down, SUM_DOWN), each(sum_up, SUM_UP), LEAD)
        for r in BACK_DOWN:
            out_up[HALF + r] = w1 * in_up[r] + w0 * state[at(r), :]
            send_up(HALF + r, out_up.at[HALF + r])
        local_part()

        def back_down(r):
            value = get_down(r)
            send_down(r, in_down.at[r])
            put(r, value + w1 * in_up[r])

        def back_up(p):
            value = get_up(p)
            out_up[p] = value + w0 * state[at(p), :]
            send_up(p, out_up.at[p])
            put(p, value)

        in_turn(each(back_down, BACK_DOWN), each(back_up, BACK_UP), LEAD + 1)

    q_turned = product(q_ref[...], turn).astype(jnp.bfloat16)
    q_twice = jnp.concatenate([q_turned, q_turned], axis=1)

    def finish(t, carry):
        cols = columns(t)
        found = level[:, cols]
        high_part = found.astype(jnp.bfloat16)
        low_part = (found - high_part.astype(jnp.float32)).astype(jnp.bfloat16)
        o_ref[:, cols] = (
            acc[:, cols] + product(q_twice, jnp.concatenate([high_part, low_part], axis=0))
        ).astype(o_ref.dtype)
        return carry

    lax.fori_loop(0, full // tile, finish, 0)

    @pl.when((spot == 0) | (spot == 2))
    def _():
        arrived(in_up, up_send)

    @pl.when(spot == 1)
    def _():
        arrived(in_up.at[pl.ds(0, PIECES)], up_send)

    @pl.when(spot > 0)
    def _():
        arrived(in_down, down_send)

    @pl.when((spot == 0) | (spot == 3))
    def _():
        arrived(in_up.at[pl.ds(0, 12)], cross_send)
        for half in range(2):
            for way in range(2):
                arrived(plane_in.at[half, pl.ds(0, planes - 1)], plane_send.at[half, way])


def on_device(inputs, keys_in, queries, step_sizes, level_weights, skip_gain):
    tokens, full = inputs.shape
    n_state = keys_in.shape[1]
    planes = lax.axis_size("sx")
    rows = n_state // PIECES
    f32 = jnp.float32
    vmem = pl.BlockSpec(memory_space=pltpu.VMEM)
    dma = pltpu.SemaphoreType.DMA
    return pl.pallas_call(
        kernel,
        out_shape=jax.ShapeDtypeStruct((tokens, full), jnp.bfloat16),
        in_specs=[vmem] * 6,
        out_specs=vmem,
        scratch_shapes=[
            pltpu.VMEM((tokens, full), jnp.bfloat16),
            pltpu.VMEM((n_state, full), f32),
            pltpu.VMEM((32, full), f32),
            pltpu.VMEM((tokens, full), f32),
            pltpu.VMEM((n_state, full), f32),
            pltpu.VMEM((PIECES + HALF, rows, full), f32),
            pltpu.VMEM((PIECES, rows, full), f32),
            pltpu.VMEM((PIECES + HALF, rows, full), f32),
            pltpu.VMEM((HALF, rows, full), f32),
            pltpu.VMEM((HALF, rows, full), f32),
            pltpu.VMEM((2, GROUP, rows, full), f32),
            pltpu.VMEM((2, GROUP, rows, full), f32),
            pltpu.VMEM((2, rows, full), f32),
            pltpu.VMEM((2, rows, full), f32),
            pltpu.VMEM((2, planes, rows, full // planes), f32),
            pltpu.VMEM((2, planes, rows, full // planes), f32),
            dma, dma((PIECES + HALF,)), dma, dma((PIECES,)),
            dma, dma((2, GROUP)), dma((HALF,)), dma((2, 2)), dma((2, 2)),
        ],
        compiler_params=pltpu.CompilerParams(
            collective_id=0, has_side_effects=True, vmem_limit_bytes=48 * 2**20
        ),
        cost_estimate=pl.CostEstimate(
            flops=10 * tokens * n_state * full, bytes_accessed=4 * tokens * full, transcendentals=0
        ),
    )(inputs, keys_in, queries, step_sizes, level_weights, skip_gain.reshape(1, -1))


def solution(mesh):
    placed = (
        P(("sx", "sy"), None),
        P(("sx", "sy"), None),
        P(("sx", "sy"), None),
        P(("sx", "sy"), None),
        P(),
        P(),
    )
    return jax.shard_map(
        on_device, mesh=mesh, in_specs=placed, out_specs=P(("sx", "sy"), None), check_vma=False
    )
```
